32 devices in a mesh: groups: 2 (over x), wide: 8 (over z, y), narrow: 2 (over core).
Axes of the slice: x: 2, y: 2, z: 4, core: 2. Of those that a mesh axis runs over, the one named last changes fastest.
Arguments:
- plume_state: bfloat16 [64, 32, 128, 128], P('groups', 'wide', 'narrow'), parts along dimension 0, may hold values from -6 to 6
- spectral_weight: bfloat16 [2, 288, 24, 32, 64], P('narrow', 'wide'), may hold values from -0.75 to 0.75
- channel_mixer: bfloat16 [32, 32], replicated, may hold values from -1 to 1
- channel_bias: float32 [32], replicated, may hold values from -3 to 3
- upstream_grad: bfloat16 [64, 32, 128, 128], P('groups', 'wide', 'narrow'), parts along dimension 0, may hold values from -6 to 6
Outputs:
- layer_out: bfloat16 [64, 32, 128, 128], P('groups', 'wide', 'narrow'), parts along dimension 0
- state_grad: bfloat16 [64, 32, 128, 128], P('groups', 'wide', 'narrow'), parts along dimension 0
- weight_grad: float32 [2, 288, 48, 32, 64], P('narrow', 'wide', 'groups'), parts along dimension 2
The draws below stay inside these ranges and needn't reach their ends.
There are 2 independent parts, one for each index of `groups`. The reference program is written for one: setup_inputs(seed, part) draws one part's arguments, and reference() takes and returns one part's arrays. A program takes and returns all parts, laid end to end along the dimension named above; an argument that names none is the same for every part. Nothing has to cross between parts.
All inputs are finite; a program needn't handle non-finite values.
Results may differ from the reference program's by a relative error of at most 0.015.
Values may be sent and summed in bfloat16 or wider, within the bound.
A program may use at most 128 MiB of HBM per device.

```python
import math
import jax
import jax.numpy as jnp

C = 32
MX = 24
MY = 24
MZ = 24
NZ = 128
BATCH = 1
NX = 32
NY = 128
KZH = 12
N_NARROW = 2


def levels(own_key, extent, shards, low, largest):
    gain, own = 1.0, jax.random.fold_in(own_key, 6)
    for position, parts in shards:
        steps = jnp.exp(jax.random.uniform(jax.random.fold_in(own, position), (parts,), jnp.float32, low / len(shards), largest / len(shards)))
        gain = gain * jnp.repeat(steps, extent[position] // parts).reshape([-1 if axis == position else 1 for axis in range(len(extent))])
    return gain


def bell_draw(key, shape, scale, most, pieces=(), held_as=jnp.bfloat16):
    entries = jax.random.normal(key, shape, jnp.float32) * scale
    if len(pieces) > 0:
        entries = levels(key, shape, pieces, -0.22, 0.18) * entries
    return jnp.clip(entries, min=-most, max=most).astype(held_as)


def setup_inputs(seed: int = 0, part: int = 0) -> dict:
    splits = jax.random.split(jax.random.key(seed), 6)
    own_keys = jax.random.split(jax.random.fold_in(splits[5], part), 6)
    return {
        "plume_state": bell_draw(own_keys[0], (BATCH * C, NX, NY, NZ), 1.0, 6.0, ((1, 8), (2, 2))),
        "spectral_weight": bell_draw(splits[1], (N_NARROW, KZH * MY, MX, C, 2 * C), (2 * C) ** -0.5, 0.75, ((0, 2), (1, 8))),
        "channel_mixer": bell_draw(splits[2], (C, C), C ** -0.5, 1.0),
        "channel_bias": bell_draw(splits[3], (C,), 0.5, 3.0, (), jnp.float32),
        "upstream_grad": bell_draw(own_keys[4], (BATCH * C, NX, NY, NZ), 1.0, 6.0, ((1, 8), (2, 2))),
    }


def contract(pattern, operand, factor):
    return jnp.einsum(pattern, operand.astype(jnp.float32), factor.astype(jnp.float32))

def mode_freq(mode_count):
    positions = jnp.arange(mode_count, dtype=jnp.int32)
    return jnp.where(positions < mode_count // 2, positions, positions - mode_count)

def phase_grid(frequency, point_count):
    places = jnp.arange(point_count, dtype=jnp.int32)
    phases = jnp.mod(frequency[:, None] * places[None, :], point_count)
    return phases.astype(jnp.float32) * (2.0 * math.pi / point_count)

def complex_table(point_count, mode_count, sign_value, scaling):
    angles = phase_grid(mode_freq(mode_count), point_count)
    real_part = jnp.cos(angles) * scaling
    imag_part = jnp.sin(angles) * (sign_value * scaling)
    upper_half = jnp.stack([real_part, -imag_part], axis=-1)
    lower_half = jnp.stack([imag_part, real_part], axis=-1)
    return jnp.stack([upper_half, lower_half], axis=0).astype(jnp.bfloat16)

def spread_table(point_count, mode_count, sign_value, scaling):
    return jnp.transpose(complex_table(point_count, mode_count, sign_value, scaling), (0, 2, 1, 3))

def real_table(point_count, mode_count, first_weight, other_weight):
    positions = jnp.arange(mode_count, dtype=jnp.int32)
    angles = phase_grid(positions, point_count)
    weighting = jnp.where(positions == 0, first_weight, other_weight)[:, None]
    return jnp.stack([jnp.cos(angles) * weighting, -jnp.sin(angles) * weighting], axis=0).astype(jnp.bfloat16)

def mix_modes(spectrum, weights, samples):
    channels = weights.shape[2]
    grouped = spectrum.reshape(spectrum.shape[0], spectrum.shape[1], 2, samples, channels)
    product = contract('kmsbi,kmiv->kmsbv', grouped, weights)
    real_part = product[:, :, 0, :, :channels] - product[:, :, 1, :, channels:]
    imag_part = product[:, :, 0, :, channels:] + product[:, :, 1, :, :channels]
    return jnp.stack([real_part, imag_part], axis=2).reshape(spectrum.shape)

def spectral_grads(spectrum, grad_modes, weights, samples):
    channels = weights.shape[2]
    grouped = (spectrum.shape[0], spectrum.shape[1], 2, samples, channels)
    operand = spectrum.reshape(grouped)
    factor = grad_modes.reshape(grouped)
    turned = jnp.stack([factor[:, :, 1], -factor[:, :, 0]], axis=2)
    real_part = contract('kmsbi,kmsbo->kmio', operand, factor)
    imag_part = contract('kmsbi,kmsbo->kmio', operand, turned)
    weight_grad = jnp.concatenate([real_part, imag_part], axis=-1)
    stacked = jnp.stack([jnp.concatenate([factor[:, :, 0], factor[:, :, 1]], axis=-1), jnp.concatenate([factor[:, :, 1], -factor[:, :, 0]], axis=-1)], axis=2)
    grad_coeff = contract('kmiv,kmsbv->kmsbi', weights, stacked).reshape(spectrum.shape)
    return (weight_grad, grad_coeff)

def channel_term(field, mixer, pattern, samples):
    grouped = field.reshape(samples, mixer.shape[0], -1)
    return contract(pattern, mixer, grouped)

def reference(plume_state, spectral_weight, channel_mixer, channel_bias, upstream_grad):
    samples = plume_state.shape[0] // C
    z_forward = real_table(NZ, MZ, 1.0 / math.sqrt(NZ), 1.0 / math.sqrt(NZ))
    z_inverse = real_table(NZ, MZ, 1.0 / math.sqrt(2 * MZ), 2.0 / math.sqrt(2 * MZ))
    forward_y = complex_table(NY, MY, -1.0, 1.0 / math.sqrt(NY))
    forward_x = complex_table(NX, MX, -1.0, 1.0 / math.sqrt(NX))
    inverse_y = spread_table(NY, MY, 1.0, 1.0 / math.sqrt(MY))
    inverse_x = spread_table(NX, MX, 1.0, 1.0 / math.sqrt(MX))
    dual_fy = spread_table(NY, MY, 1.0, 1.0 / math.sqrt(NY))
    dual_fx = spread_table(NX, MX, 1.0, 1.0 / math.sqrt(NX))
    dual_iy = complex_table(NY, MY, -1.0, 1.0 / math.sqrt(MY))
    dual_ix = complex_table(NX, MX, -1.0, 1.0 / math.sqrt(MX))
    weights = spectral_weight.reshape(MZ * MY, MX, C, 2 * C)
    coeff_z = contract('skz,cabz->kscab', z_forward, plume_state).astype(jnp.bfloat16)
    coeff_y = contract('kscab,rqbs->kqrca', coeff_z, forward_y).astype(jnp.bfloat16)
    spectrum = contract('kqsca,rmas->kqmrc', coeff_y, forward_x).astype(jnp.bfloat16)
    spectrum = spectrum.reshape(MZ * MY, MX, 2, samples * C)
    mixed_modes = mix_modes(spectrum, weights, samples).astype(jnp.bfloat16)
    mixed_modes = mixed_modes.reshape(MZ, MY, MX, 2, samples * C)
    back_x = contract('kqmsc,rams->kqrca', mixed_modes, inverse_x).astype(jnp.bfloat16)
    back_y = contract('kqsca,rbqs->krcab', back_x, inverse_y).astype(jnp.bfloat16)
    spectral = contract('kscab,skz->cabz', back_y, z_inverse)
    linear = channel_term(plume_state, channel_mixer, 'io,bip->bop', samples) + channel_bias[None, :, None]
    pre_act = spectral + linear.reshape(spectral.shape)
    layer_out = jax.nn.gelu(pre_act).astype(jnp.bfloat16)
    pullback = jax.vjp(jax.nn.gelu, pre_act)[1]
    slope_grad = pullback(upstream_grad.astype(jnp.float32))[0].astype(jnp.bfloat16)
    grad_z = contract('skz,cabz->kscab', z_inverse, slope_grad).astype(jnp.bfloat16)
    grad_y = contract('kscab,rqbs->kqrca', grad_z, dual_iy).astype(jnp.bfloat16)
    grad_modes = contract('kqsca,rmas->kqmrc', grad_y, dual_ix).astype(jnp.bfloat16)
    grad_modes = grad_modes.reshape(MZ * MY, MX, 2, samples * C)
    weight_grad, grad_coeff = spectral_grads(spectrum, grad_modes, weights, samples)
    grad_coeff = grad_coeff.astype(jnp.bfloat16).reshape(MZ, MY, MX, 2, samples * C)
    grad_x = contract('kqmsc,rams->kqrca', grad_coeff, dual_fx).astype(jnp.bfloat16)
    grad_yb = contract('kqsca,rbqs->krcab', grad_x, dual_fy).astype(jnp.bfloat16)
    spatial_grad = contract('kscab,skz->cabz', grad_yb, z_forward)
    mixer_grad = channel_term(slope_grad, channel_mixer, 'io,bop->bip', samples)
    state_grad = (spatial_grad + mixer_grad.reshape(spatial_grad.shape)).astype(jnp.bfloat16)
    return (layer_out, state_grad, weight_grad.reshape(spectral_weight.shape))
```

```python
import functools
import math

import jax
import jax.numpy as jnp
import numpy as np
from jax import lax
from jax.experimental import pallas as pl
from jax.experimental.pallas import tpu as pltpu
from jax.sharding import PartitionSpec as P

C = 32
MX = 24
MY = 24
MZ = 24
OCT = 8
F32 = jnp.float32
BF16 = jnp.bfloat16
VMEM_LIMIT = 50 * 1024 * 1024


def mm(left, right):
    return jnp.dot(left, right, preferred_element_type=F32)


def mm_nt(left, right):
    return lax.dot_general(left, right, (((1,), (1,)), ((), ())), preferred_element_type=F32)


def const(array):
    return jnp.asarray(np.asarray(array, np.float32)).astype(BF16)


def phases(points, frequency):
    turns = np.mod(frequency[:, None] * np.arange(points)[None, :], points)
    return turns.astype(np.float64) * (2.0 * math.pi / points)


def wave(points, modes, sign, scale):
    index = np.arange(modes)
    angles = phases(points, np.where(index < modes // 2, index, index - modes))
    return np.cos(angles) * scale, sign * np.sin(angles) * scale


def y_forward_table(points, parts, cells_x, scale):
    real, imag = wave(points, MY, -1.0, scale)
    local = np.stack([real, imag]).reshape(2, MY, parts, points // parts)
    table = np.einsum("sqnb,ac->nsaqcb", local, np.eye(cells_x))
    return const(table.reshape(parts, 2 * cells_x * MY, -1))


def y_inverse_table(points, parts, cells_x, scale):
    real, imag = wave(points, MY, 1.0, scale)
    local = np.stack([real, -imag]).reshape(2, MY, parts, points // parts)
    table = np.einsum("sqnb,ac->ncbsaq", local, np.eye(cells_x))
    return const(table.reshape(parts, -1, 2 * cells_x * MY))


def z_parts(points, first, other):
    angles = phases(points, np.arange(MZ))
    weight = np.where(np.arange(MZ) == 0, first, other)[:, None]
    return np.cos(angles) * weight, np.sin(angles) * weight


def z_forward_table(points, first, other):
    cos, sin = z_parts(points, first, other)
    table = np.zeros((2 * points, 128))
    table[:points, :MZ] = cos.T
    table[points:, :MZ] = sin.T
    table[:points, MZ : 2 * MZ] = -sin.T
    table[points:, MZ : 2 * MZ] = cos.T
    return const(table)


def z_inverse_table(points, first, other):
    cos, sin = z_parts(points, first, other)
    table = np.zeros((128, 2 * points))
    table[:MZ, :points] = cos
    table[MZ : 2 * MZ, :points] = -sin
    table[:MZ, points:] = sin
    table[MZ : 2 * MZ, points:] = cos
    return const(table)


def x_blocks(points, sign, scale):
    real, imag = wave(points, MX, sign, scale)
    table = np.stack([np.stack([real, -imag]), np.stack([imag, real])])
    return table.reshape(2, 2, MX // OCT, OCT, points)


def x_forward_table(points, parts, wide, cells_x, scale, turned=False):
    table = x_blocks(points, -1.0, scale)
    if turned:
        table = np.stack([table[1], -table[0]])
    table = table.reshape(2, 2, MX // OCT, OCT, wide, cells_x)
    table = np.broadcast_to(table, (parts,) + table.shape)
    table = np.einsum("nrsjmwa->ajrmnws", table)
    return table.reshape(cells_x * 2 * MX, parts * wide * 2)


def x_inverse_table(points, wide, cells_x, scale):
    table = x_blocks(points, 1.0, scale).reshape(2, 2, MX // OCT, OCT, wide, cells_x)
    return const(np.einsum("rsjmwa->awrjsm", table).reshape(cells_x * wide * 2, 2 * MX))


def lane_masks(cells_x):
    lanes = np.arange(C * cells_x) % cells_x
    masks = np.zeros((8, C * cells_x), np.float32)
    masks[:cells_x] = lanes[None, :] == np.arange(cells_x)[:, None]
    return jnp.asarray(masks)


def octet_of_rows():
    return np.arange(2 * MX) % OCT


def forward_transform(get_rows, y_table, z_table, out_ref, held, turned, cells_x):
    rows = cells_x * MY
    together = 4

    def channels(step, carry):
        for offset in range(together):
            c = step * together + offset
            part = mm(y_table, get_rows(c)).astype(BF16)
            both = jnp.concatenate([part[:rows], part[rows:]], axis=1)
            held[pl.ds(pl.multiple_of(c * rows, 8), rows), :] = mm(both, z_table)
        return carry

    lax.fori_loop(0, C // together, channels, 0)
    for q in range(MY):
        block = held[pl.ds(q, C * cells_x, stride=MY), :]
        turned[pl.ds(q, 2 * MZ, stride=MY), :] = block.T[: 2 * MZ]
    pairs = out_ref.shape[2]
    for target in range(out_ref.shape[0]):
        for part in range(2):
            begin = part * MZ * MY + target * pairs
            out_ref[target, part] = turned[begin : begin + pairs, :].astype(BF16)


def inverse_transform(in_ref, y_table, z_table, put_rows, held, turned, cells_x):
    rows = cells_x * MY
    together = 4
    pairs = in_ref.shape[2]
    points = z_table.shape[1] // 2
    lanes = held.shape[1]
    for source in range(in_ref.shape[0]):
        for part in range(2):
            begin = part * MZ * MY + source * pairs
            turned[begin : begin + pairs, :] = in_ref[source, part].astype(F32)
    for q in range(MY):
        block = turned[pl.ds(q, 2 * MZ, stride=MY), :]
        padded = jnp.concatenate([block, jnp.zeros((lanes - 2 * MZ, block.shape[1]), F32)], axis=0)
        held[pl.ds(q, C * cells_x, stride=MY), :] = padded.T

    def channels(step, carry):
        for offset in range(together):
            c = step * together + offset
            block = held[pl.ds(pl.multiple_of(c * rows, 8), rows), :].astype(BF16)
            both = mm(block, z_table).astype(BF16)
            stacked = jnp.concatenate([both[:, :points], both[:, points:]], axis=0)
            put_rows(c, mm(y_table, stacked))
        return carry

    lax.fori_loop(0, C // together, channels, 0)


def forward_kernel(cells_x, field, y_tables, z_table, out_ref, held, turned):
    y_table = y_tables[lax.axis_index("narrow")]
    forward_transform(
        lambda c: field[c], y_table, z_table[...], out_ref, held, turned, cells_x
    )


def tall_mixer(spread, mixer, mask):
    wide = mm(spread, mixer).astype(BF16)
    return (mm_nt(wide, spread).astype(BF16)) * mask


def mixed_field(table, field, begin, band):
    depth = field.shape[2]
    blocks = [field[:, pl.ds(begin + half * band, band), :] for half in range(2)]
    flat = [block.reshape(C * band, depth) for block in blocks]
    product = mm(table, jnp.concatenate(flat, axis=1))
    return [product[:, half * depth : (half + 1) * depth].reshape(C, band, depth) for half in range(2)]


def middle_kernel(
    cells_x, band, arrived, field, upstream, spread, mixer, mask, bias,
    y_back, z_back, y_dual, z_dual,
    layer_out, slope, out_ref, held, turned, spectral,
):
    me = lax.axis_index("narrow")

    def put(c, rows):
        spectral[c] = rows

    inverse_transform(arrived, y_back[me], z_back[...], put, held, turned, cells_x)
    table = tall_mixer(spread[...], mixer[...], mask[...])
    offset = bias[...][:, :, None]
    alpha = math.sqrt(2.0 / math.pi)
    cubic = alpha * 0.044715

    def bands(step, carry):
        begin = pl.multiple_of(step * 2 * band, 2 * band)
        linear = mixed_field(table, field, begin, band)
        for half in range(2):
            where = pl.ds(begin + half * band, band)
            v = spectral[:, where, :] + (linear[half] + offset)
            square = v * v
            t = jnp.tanh(v * (alpha + cubic * square))
            gate = 0.5 + 0.5 * t
            layer_out[:, where, :] = (v * gate).astype(BF16)
            rise = (0.5 * v) * (1.0 - t * t) * (alpha + (3.0 * cubic) * square)
            grad = upstream[:, where, :].astype(F32) * (gate + rise)
            slope[:, where, :] = grad.astype(BF16)
        return carry

    lax.fori_loop(0, field.shape[1] // (2 * band), bands, 0)
    forward_transform(
        lambda c: slope[c], y_dual[me], z_dual[...], out_ref, held, turned, cells_x
    )


def final_kernel(
    cells_x, band, arrived, slope, spread, mixer, mask, y_back, z_back, out_ref, held, turned,
    spectral,
):
    me = lax.axis_index("narrow")

    def put(c, rows):
        spectral[c] = rows

    inverse_transform(arrived, y_back[me], z_back[...], put, held, turned, cells_x)
    table = tall_mixer(spread[...], mixer[...], mask[...])

    def bands(step, carry):
        begin = pl.multiple_of(step * 2 * band, 2 * band)
        linear = mixed_field(table, slope, begin, band)
        for half in range(2):
            where = pl.ds(begin + half * band, band)
            out_ref[:, where, :] = (spectral[:, where, :] + linear[half]).astype(BF16)
        return carry

    lax.fori_loop(0, slope.shape[1] // (2 * band), bands, 0)


def unpack_pairs(arrived, loose):
    pairs = arrived.shape[2]
    for source in range(arrived.shape[0]):
        for part in range(2):
            begin = (source * 2 + part) * pairs
            loose[begin : begin + pairs, :] = arrived[source, part].astype(F32)


def pick_cells(product, masks, cells_x, begin=0):
    rows = product.shape[0] // cells_x if begin is None else 2 * MX
    total = None
    for a in range(cells_x):
        low = (begin or 0) + a * rows
        term = product[low : low + rows] * masks[a : a + 1]
        total = term if total is None else total + term
    return total


def send_pairs(gathered, out_ref, wide):
    pairs = out_ref.shape[2]
    for target in range(out_ref.shape[0]):
        for part in range(2):
            begin = ((target % wide) * 2 + part) * pairs
            out_ref[target, part] = gathered[begin : begin + pairs, :].astype(BF16)


def mix_kernel(
    cells_x, wide, group, arrived, weights, x_table, x_back, masks, copies, octets, picks,
    out_ref, spectrum_t, loose, gathered,
):
    step = pl.program_id(0)
    pairs = arrived.shape[2]
    sources = arrived.shape[0] * 2

    @pl.when(step == 0)
    def _():
        unpack_pairs(arrived, loose)

    lanes = masks[...]
    for offset in range(group):
        pair = step * group + offset
        data = loose[pl.ds(pair, sources, stride=pairs), :].astype(BF16)
        chosen = pick_cells(mm(x_table[...], data), lanes, cells_x).astype(BF16)
        spectrum_t[offset] = mm_nt(picks[...], chosen).astype(BF16)
        diagonal = mm(chosen, copies[...]).astype(BF16) * octets[...]
        rows = []
        for j in range(MX // OCT):
            low = offset * MX * C + j * OCT * C
            product = mm(diagonal[2 * OCT * j : 2 * OCT * (j + 1)], weights[low : low + OCT * C, :])
            top, bottom = product[:OCT], product[OCT:]
            rows.append(top[:, :C] - bottom[:, C:])
            rows.append(top[:, C:] + bottom[:, :C])
        mixed = jnp.concatenate(rows, axis=0).astype(BF16)
        back = mm(x_back[...], mm(mixed, picks[...]).astype(BF16))
        gathered[pl.ds(pair, 2 * wide, stride=pairs), :] = pick_cells(back, lanes, cells_x, None)

    @pl.when(step == pl.num_programs(0) - 1)
    def _():
        send_pairs(gathered, out_ref, wide)


def grad_kernel(
    cells_x, wide, group, arrived, weights, spectrum_t, x_table, x_back, masks, sides, octets,
    octets_t, shrink, out_ref, weight_grad, loose, gathered,
):
    step = pl.program_id(0)
    pairs = arrived.shape[2]
    sources = arrived.shape[0] * 2

    @pl.when(step == 0)
    def _():
        unpack_pairs(arrived, loose)

    lanes = masks[...]
    for offset in range(group):
        pair = step * group + offset
        data = loose[pl.ds(pair, sources, stride=pairs), :].astype(BF16)
        product = mm(x_table[...], data)
        straight = pick_cells(product, lanes, cells_x).astype(BF16)
        turned = pick_cells(product, lanes, cells_x, 2 * MX * cells_x).astype(BF16)
        stacked = mm(jnp.concatenate([straight, turned], axis=1), sides[...]).astype(BF16)
        tall = jnp.concatenate([spectrum_t[offset]] * MX, axis=0) * octets_t[...]
        low = offset * MX * C
        weight_grad[low : low + MX * C, :] = mm(tall, stacked)
        rows = []
        for j in range(MX // OCT):
            block = weights[low + j * OCT * C : low + (j + 1) * OCT * C, :]
            rows.append(mm_nt(stacked[2 * OCT * j : 2 * OCT * (j + 1)], block))
        coeff = jnp.concatenate(rows, axis=0).astype(BF16) * octets[...]
        back = mm(x_back[...], mm(coeff, shrink[...]).astype(BF16))
        gathered[pl.ds(pair, 2 * wide, stride=pairs), :] = pick_cells(back, lanes, cells_x, None)

    @pl.when(step == pl.num_programs(0) - 1)
    def _():
        send_pairs(gathered, out_ref, wide)


def exchange(blocks):
    return lax.all_to_all(blocks, ("narrow", "wide"), split_axis=0, concat_axis=0, tiled=True)


def whole_spec(shape):
    return pl.BlockSpec(shape, lambda *_: (0,) * len(shape))


def body(plume_state, spectral_weight, channel_mixer, channel_bias, upstream_grad):
    row_count, cells_x, cells_y, depth = plume_state.shape
    wide = lax.axis_size("wide")
    parts = lax.axis_size("narrow")
    span_x = cells_x * wide
    span_y = cells_y * parts
    flat = cells_x * cells_y
    lanes = C * cells_x
    targets = parts * wide
    pairs = spectral_weight.shape[1]
    band = 16
    group = max(g for g in (4, 3, 2, 1) if pairs % g == 0)
    down = 1.0 / math.sqrt(depth)
    z_fwd = z_forward_table(depth, down, down)
    z_fwd_back = z_inverse_table(depth, down, down)
    first, other = 1.0 / math.sqrt(2 * MZ), 2.0 / math.sqrt(2 * MZ)
    z_inv = z_inverse_table(depth, first, other)
    z_inv_back = z_forward_table(depth, first, other)
    y_fwd = y_forward_table(span_y, parts, cells_x, 1.0 / math.sqrt(span_y))
    y_inv = y_inverse_table(span_y, parts, cells_x, 1.0 / math.sqrt(MY))
    y_dual_inv = y_forward_table(span_y, parts, cells_x, 1.0 / math.sqrt(MY))
    y_dual_fwd = y_inverse_table(span_y, parts, cells_x, 1.0 / math.sqrt(span_y))
    x_fwd = const(x_forward_table(span_x, parts, wide, cells_x, 1.0 / math.sqrt(span_x)))
    x_inv = x_inverse_table(span_x, wide, cells_x, 1.0 / math.sqrt(MX))
    scale = 1.0 / math.sqrt(MX)
    x_dual_inv = const(
        np.concatenate(
            [x_forward_table(span_x, parts, wide, cells_x, scale, turn) for turn in (False, True)]
        )
    )
    x_dual_fwd = x_inverse_table(span_x, wide, cells_x, 1.0 / math.sqrt(span_x))
    masks = lane_masks(cells_x)
    lane_c = np.arange(lanes) // cells_x
    picks_np = np.arange(C)[:, None] == lane_c[None, :]
    picks = const(picks_np)
    copies_np = np.tile(picks_np.T, (1, OCT))
    copies = const(copies_np)
    shrink = const(copies_np.T)
    octets_np = octet_of_rows()[:, None] == (np.arange(OCT * C) // C)[None, :]
    octets = const(octets_np)
    row_mode = (np.arange(2 * MX) // (2 * OCT)) * OCT + np.arange(2 * MX) % OCT
    octets_t = const((np.arange(MX * C) // C)[:, None] == row_mode[None, :])
    sides_np = np.zeros((2 * lanes, 2 * C))
    sides_np[:lanes, :C] = picks_np.T
    sides_np[lanes:, C:] = picks_np.T
    sides = const(sides_np)
    spread = const((np.arange(C * band) // band)[:, None] == np.arange(C)[None, :])
    band_index = np.arange(C * band) % band
    band_mask = const(band_index[:, None] == band_index[None, :])

    params = pltpu.CompilerParams(vmem_limit_bytes=VMEM_LIMIT)
    message = jax.ShapeDtypeStruct((targets, 2, pairs, lanes), BF16)
    held = pltpu.VMEM((lanes * MY, 128), F32)
    turned = pltpu.VMEM((2 * MZ * MY, lanes), F32)
    spectral = pltpu.VMEM((C, flat, depth), F32)
    loose = pltpu.VMEM((targets * 2 * pairs, lanes), F32)
    gathered = pltpu.VMEM((2 * wide * pairs, lanes), F32)
    field = plume_state.reshape(C, flat, depth)
    upstream = upstream_grad.reshape(C, flat, depth)
    weights = spectral_weight.reshape(pairs * MX * C, 2 * C)
    field_shape = jax.ShapeDtypeStruct((C, flat, depth), BF16)
    weight_spec = pl.BlockSpec((group * MX * C, 2 * C), lambda i: (i, 0))
    spectrum_spec = pl.BlockSpec((group, C, 2 * MX), lambda i: (i, 0, 0))

    sent = pl.pallas_call(
        functools.partial(forward_kernel, cells_x),
        out_shape=message,
        scratch_shapes=[held, turned],
        compiler_params=params,
    )(field, y_fwd, z_fwd)
    arrived = exchange(sent)

    operands = (x_fwd, x_inv, masks, copies, octets, picks)
    sent, spectrum_t = pl.pallas_call(
        functools.partial(mix_kernel, cells_x, wide, group),
        grid=(pairs // group,),
        in_specs=[whole_spec(message.shape), weight_spec] + [whole_spec(t.shape) for t in operands],
        out_specs=[whole_spec(message.shape), spectrum_spec],
        out_shape=[message, jax.ShapeDtypeStruct((pairs, C, 2 * MX), BF16)],
        scratch_shapes=[loose, gathered],
        compiler_params=params,
    )(arrived, weights, *operands)
    arrived = exchange(sent)

    layer_out, slope, sent = pl.pallas_call(
        functools.partial(middle_kernel, cells_x, band),
        out_shape=[field_shape, field_shape, message],
        scratch_shapes=[held, turned, spectral],
        compiler_params=params,
    )(
        arrived, field, upstream, spread, channel_mixer.T, band_mask, channel_bias[:, None],
        y_inv, z_inv, y_dual_inv, z_inv_back,
    )
    arrived = exchange(sent)

    operands = (x_dual_inv, x_dual_fwd, masks, sides, octets, octets_t, shrink)
    sent, weight_grad = pl.pallas_call(
        functools.partial(grad_kernel, cells_x, wide, group),
        grid=(pairs // group,),
        in_specs=[whole_spec(message.shape), weight_spec, spectrum_spec]
        + [whole_spec(t.shape) for t in operands],
        out_specs=[whole_spec(message.shape), weight_spec],
        out_shape=[message, jax.ShapeDtypeStruct(weights.shape, F32)],
        scratch_shapes=[loose, gathered],
        compiler_params=params,
    )(arrived, weights, spectrum_t, *operands)
    arrived = exchange(sent)

    state_grad = pl.pallas_call(
        functools.partial(final_kernel, cells_x, band),
        out_shape=field_shape,
        scratch_shapes=[held, turned, spectral],
        compiler_params=params,
    )(arrived, slope, spread, channel_mixer, band_mask, y_dual_fwd, z_fwd_back)
    return (
        layer_out.reshape(plume_state.shape),
        state_grad.reshape(plume_state.shape),
        weight_grad.reshape(spectral_weight.shape),
    )


def solution(mesh):
    in_specs = (
        P("groups", "wide", "narrow", None),
        P("narrow", "wide", None, None, None),
        P(),
        P(),
        P("groups", "wide", "narrow", None),
    )
    out_specs = (
        P("groups", "wide", "narrow", None),
        P("groups", "wide", "narrow", None),
        P("narrow", "wide", "groups", None, None),
    )
    return jax.shard_map(body, mesh=mesh, in_specs=in_specs, out_specs=out_specs, check_vma=False)
```

```python
import functools
import math

import jax
import jax.numpy as jnp
import numpy as np
from jax import lax
from jax.experimental import pallas as pl
from jax.experimental.pallas import tpu as pltpu
from jax.sharding import PartitionSpec as P

C = 32
MX = 24
MY = 24
MZ = 24
OCT = 8
F32 = jnp.float32
BF16 = jnp.bfloat16
VMEM_LIMIT = 50 * 1024 * 1024


def mm(left, right):
    return jnp.dot(left, right, preferred_element_type=F32)


def mm_nt(left, right):
    return lax.dot_general(left, right, (((1,), (1,)), ((), ())), preferred_element_type=F32)


def const(array):
    return jnp.asarray(np.asarray(array, np.float32)).astype(BF16)


def phases(points, frequency):
    turns = np.mod(frequency[:, None] * np.arange(points)[None, :], points)
    return turns.astype(np.float64) * (2.0 * math.pi / points)


def wave(points, modes, sign, scale):
    index = np.arange(modes)
    angles = phases(points, np.where(index < modes // 2, index, index - modes))
    return np.cos(angles) * scale, sign * np.sin(angles) * scale


def y_forward_table(points, parts, cells_x, scale):
    real, imag = wave(points, MY, -1.0, scale)
    local = np.stack([real, imag]).reshape(2, MY, parts, points // parts)
    table = np.einsum("sqnb,ac->nsaqcb", local, np.eye(cells_x))
    return const(table.reshape(parts, 2 * cells_x * MY, -1))


def y_inverse_table(points, parts, cells_x, scale):
    real, imag = wave(points, MY, 1.0, scale)
    local = np.stack([real, -imag]).reshape(2, MY, parts, points // parts)
    table = np.einsum("sqnb,ac->ncbsaq", local, np.eye(cells_x))
    return const(table.reshape(parts, -1, 2 * cells_x * MY))


def z_parts(points, first, other):
    angles = phases(points, np.arange(MZ))
    weight = np.where(np.arange(MZ) == 0, first, other)[:, None]
    return np.cos(angles) * weight, np.sin(angles) * weight


def z_forward_table(points, first, other):
    cos, sin = z_parts(points, first, other)
    table = np.zeros((2 * points, 128))
    table[:points, :MZ] = cos.T
    table[points:, :MZ] = sin.T
    table[:points, MZ : 2 * MZ] = -sin.T
    table[points:, MZ : 2 * MZ] = cos.T
    return const(table)


def z_inverse_table(points, first, other):
    cos, sin = z_parts(points, first, other)
    table = np.zeros((128, 2 * points))
    table[:MZ, :points] = cos
    table[MZ : 2 * MZ, :points] = -sin
    table[:MZ, points:] = sin
    table[MZ : 2 * MZ, points:] = cos
    return const(table)


def x_blocks(points, sign, scale):
    real, imag = wave(points, MX, sign, scale)
    table = np.stack([np.stack([real, -imag]), np.stack([imag, real])])
    return table.reshape(2, 2, MX // OCT, OCT, points)


def x_forward_table(points, parts, wide, cells_x, scale, turned=False):
    table = x_blocks(points, -1.0, scale)
    if turned:
        table = np.stack([table[1], -table[0]])
    table = table.reshape(2, 2, MX // OCT, OCT, wide, cells_x)
    table = np.broadcast_to(table, (parts,) + table.shape)
    table = np.einsum("nrsjmwa->jrmanws", table)
    return table.reshape(2 * MX, cells_x * parts * wide * 2)


def x_inverse_table(points, wide, cells_x, scale):
    table = x_blocks(points, 1.0, scale).reshape(2, 2, MX // OCT, OCT, wide, cells_x)
    return const(np.einsum("rsjmwa->wrajsm", table).reshape(wide * 2, cells_x * 2 * MX))


def cell_mask(cells_x, rows):
    owner = np.arange(cells_x * rows) // rows
    return const(owner[:, None] == (np.arange(C * cells_x) % cells_x)[None, :])


def octet_of_rows():
    return np.arange(2 * MX) % OCT


def forward_transform(get_rows, y_table, z_table, out_ref, held, turned, cells_x):
    rows = cells_x * MY
    together = 4

    def channels(step, carry):
        for offset in range(together):
            c = step * together + offset
            part = mm(y_table, get_rows(c)).astype(BF16)
            both = jnp.concatenate([part[:rows], part[rows:]], axis=1)
            held[pl.ds(pl.multiple_of(c * rows, 8), rows), :] = mm(both, z_table)
        return carry

    lax.fori_loop(0, C // together, channels, 0)
    for q in range(MY):
        block = held[pl.ds(q, C * cells_x, stride=MY), :]
        turned[pl.ds(q, 2 * MZ, stride=MY), :] = block.T[: 2 * MZ]
    pairs = out_ref.shape[2]
    for target in range(out_ref.shape[0]):
        for part in range(2):
            begin = part * MZ * MY + target * pairs
            out_ref[target, part] = turned[begin : begin + pairs, :].astype(BF16)


def inverse_transform(in_ref, y_table, z_table, put_rows, held, turned, cells_x):
    rows = cells_x * MY
    together = 4
    pairs = in_ref.shape[2]
    points = z_table.shape[1] // 2
    lanes = held.shape[1]
    for source in range(in_ref.shape[0]):
        for part in range(2):
            begin = part * MZ * MY + source * pairs
            turned[begin : begin + pairs, :] = in_ref[source, part].astype(F32)
    for q in range(MY):
        block = turned[pl.ds(q, 2 * MZ, stride=MY), :]
        padded = jnp.concatenate([block, jnp.zeros((lanes - 2 * MZ, block.shape[1]), F32)], axis=0)
        held[pl.ds(q, C * cells_x, stride=MY), :] = padded.T

    def channels(step, carry):
        for offset in range(together):
            c = step * together + offset
            block = held[pl.ds(pl.multiple_of(c * rows, 8), rows), :].astype(BF16)
            both = mm(block, z_table).astype(BF16)
            stacked = jnp.concatenate([both[:, :points], both[:, points:]], axis=0)
            put_rows(c, mm(y_table, stacked))
        return carry

    lax.fori_loop(0, C // together, channels, 0)


def forward_kernel(cells_x, field, y_tables, z_table, out_ref, held, turned):
    y_table = y_tables[lax.axis_index("narrow")]
    forward_transform(
        lambda c: field[c], y_table, z_table[...], out_ref, held, turned, cells_x
    )


def tall_mixer(spread, mixer, mask):
    wide = mm(spread, mixer).astype(BF16)
    return (mm_nt(wide, spread).astype(BF16)) * mask


def mixed_field(table, field, begin, band):
    depth = field.shape[2]
    blocks = [field[:, pl.ds(begin + half * band, band), :] for half in range(2)]
    flat = [block.reshape(C * band, depth) for block in blocks]
    product = mm(table, jnp.concatenate(flat, axis=1))
    return [product[:, half * depth : (half + 1) * depth].reshape(C, band, depth) for half in range(2)]


def middle_kernel(
    cells_x, band, arrived, field, upstream, spread, mixer, mask, bias,
    y_back, z_back, y_dual, z_dual,
    layer_out, slope, out_ref, held, turned, spectral,
):
    me = lax.axis_index("narrow")

    def put(c, rows):
        spectral[c] = rows

    inverse_transform(arrived, y_back[me], z_back[...], put, held, turned, cells_x)
    table = tall_mixer(spread[...], mixer[...], mask[...])
    offset = bias[...][:, :, None]
    alpha = math.sqrt(2.0 / math.pi)
    cubic = alpha * 0.044715

    def bands(step, carry):
        begin = pl.multiple_of(step * 2 * band, 2 * band)
        linear = mixed_field(table, field, begin, band)
        for half in range(2):
            where = pl.ds(begin + half * band, band)
            v = spectral[:, where, :] + (linear[half] + offset)
            square = v * v
            t = jnp.tanh(v * (alpha + cubic * square))
            gate = 0.5 + 0.5 * t
            layer_out[:, where, :] = (v * gate).astype(BF16)
            rise = (0.5 * v) * (1.0 - t * t) * (alpha + (3.0 * cubic) * square)
            grad = upstream[:, where, :].astype(F32) * (gate + rise)
            slope[:, where, :] = grad.astype(BF16)
        return carry

    lax.fori_loop(0, field.shape[1] // (2 * band), bands, 0)
    forward_transform(
        lambda c: slope[c], y_dual[me], z_dual[...], out_ref, held, turned, cells_x
    )


def final_kernel(
    cells_x, band, arrived, slope, spread, mixer, mask, y_back, z_back, out_ref, held, turned,
    spectral,
):
    me = lax.axis_index("narrow")

    def put(c, rows):
        spectral[c] = rows

    inverse_transform(arrived, y_back[me], z_back[...], put, held, turned, cells_x)
    table = tall_mixer(spread[...], mixer[...], mask[...])

    def bands(step, carry):
        begin = pl.multiple_of(step * 2 * band, 2 * band)
        linear = mixed_field(table, slope, begin, band)
        for half in range(2):
            where = pl.ds(begin + half * band, band)
            out_ref[:, where, :] = (spectral[:, where, :] + linear[half]).astype(BF16)
        return carry

    lax.fori_loop(0, slope.shape[1] // (2 * band), bands, 0)


def unpack_pairs(arrived, loose):
    pairs = arrived.shape[2]
    for source in range(arrived.shape[0]):
        for part in range(2):
            begin = (source * 2 + part) * pairs
            loose[begin : begin + pairs, :] = arrived[source, part].astype(F32)


def to_modes(loose, x_table, cell_rows, first, group, pairs, cells_x):
    count = loose.shape[0] // pairs
    blocks = []
    for offset in range(group):
        data = loose[pl.ds(first + offset, count, stride=pairs), :].astype(BF16)
        blocks.append(jnp.concatenate([data] * cells_x, axis=0) * cell_rows)
    return mm(x_table, jnp.concatenate(blocks, axis=1)).astype(BF16)


def from_modes(modes, x_back, cell_rows, gathered, first, group, pairs, cells_x):
    rows = 2 * MX
    lanes = modes.shape[1]
    blocks = []
    for offset in range(group):
        data = modes[offset * rows : (offset + 1) * rows]
        blocks.append(jnp.concatenate([data] * cells_x, axis=0) * cell_rows)
    back = mm(x_back, jnp.concatenate(blocks, axis=1))
    for offset in range(group):
        where = pl.ds(first + offset, x_back.shape[0], stride=pairs)
        gathered[where, :] = back[:, offset * lanes : (offset + 1) * lanes]


def send_pairs(gathered, out_ref, wide):
    pairs = out_ref.shape[2]
    for target in range(out_ref.shape[0]):
        for part in range(2):
            begin = ((target % wide) * 2 + part) * pairs
            out_ref[target, part] = gathered[begin : begin + pairs, :].astype(BF16)


def per_pair(array, group, low, high):
    lanes = array.shape[1] // group
    parts = [array[low:high, n * lanes : (n + 1) * lanes] for n in range(group)]
    return jnp.concatenate(parts, axis=0)


def mix_kernel(
    cells_x, wide, group, arrived, weights, x_table, x_back, source_rows, mode_rows, copies,
    octets, picks, doubled, out_ref, spectrum_t, loose, gathered,
):
    step = pl.program_id(0)
    pairs = arrived.shape[2]
    rows = 2 * MX
    first = step * group

    @pl.when(step == 0)
    def _():
        unpack_pairs(arrived, loose)

    modes = to_modes(loose, x_table[...], source_rows[...], first, group, pairs, cells_x)
    chosen = per_pair(modes, group, 0, rows)
    mask = jnp.concatenate([octets[...]] * group, axis=0)
    diagonal = mm(chosen, copies[...]).astype(BF16) * mask
    products = []
    for n in range(group * (MX // OCT)):
        block = weights[n * OCT * C : (n + 1) * OCT * C, :]
        products.append(mm(diagonal[2 * OCT * n : 2 * OCT * (n + 1)], block))
    product = jnp.concatenate(products, axis=0).astype(BF16)
    both = mm(product, doubled[...])
    lanes = both.shape[1] // 2
    mixed = []
    for n in range(group * (MX // OCT)):
        top = both[2 * OCT * n : 2 * OCT * n + OCT]
        bottom = both[2 * OCT * n + OCT : 2 * OCT * (n + 1)]
        mixed.append(top[:, :lanes] - bottom[:, lanes:])
        mixed.append(top[:, lanes:] + bottom[:, :lanes])
    mixed = jnp.concatenate(mixed, axis=0).astype(BF16)
    from_modes(mixed, x_back[...], mode_rows[...], gathered, first, group, pairs, cells_x)
    for n in range(group):
        spectrum_t[n] = mm_nt(picks[...], chosen[n * rows : (n + 1) * rows]).astype(BF16)

    @pl.when(step == pl.num_programs(0) - 1)
    def _():
        send_pairs(gathered, out_ref, wide)


def grad_kernel(
    cells_x, wide, group, arrived, weights, spectrum_t, x_table, x_back, source_rows, mode_rows,
    sides, octets, octets_t, shrink, out_ref, weight_grad, loose, gathered,
):
    step = pl.program_id(0)
    pairs = arrived.shape[2]
    rows = 2 * MX
    first = step * group

    @pl.when(step == 0)
    def _():
        unpack_pairs(arrived, loose)

    modes = to_modes(loose, x_table[...], source_rows[...], first, group, pairs, cells_x)
    straight = per_pair(modes, group, 0, rows)
    turned = per_pair(modes, group, rows, 2 * rows)
    stacked = mm(jnp.concatenate([straight, turned], axis=1), sides[...]).astype(BF16)
    coeffs = []
    for n in range(group * (MX // OCT)):
        block = weights[n * OCT * C : (n + 1) * OCT * C, :]
        coeffs.append(mm_nt(stacked[2 * OCT * n : 2 * OCT * (n + 1)], block))
    mask = jnp.concatenate([octets[...]] * group, axis=0)
    coeff = jnp.concatenate(coeffs, axis=0).astype(BF16) * mask
    spread = mm(coeff, shrink[...]).astype(BF16)
    from_modes(spread, x_back[...], mode_rows[...], gathered, first, group, pairs, cells_x)
    for n in range(group):
        tall = jnp.concatenate([spectrum_t[n]] * MX, axis=0) * octets_t[...]
        weight_grad[n * MX * C : (n + 1) * MX * C, :] = mm(tall, stacked[n * rows : (n + 1) * rows])

    @pl.when(step == pl.num_programs(0) - 1)
    def _():
        send_pairs(gathered, out_ref, wide)


def exchange_kernel(parts, wide, sent, arrived, send_sem, recv_sem):
    count = parts * wide
    me = lax.axis_index("narrow") * wide + lax.axis_index("wide")

    def device(place):
        return {"narrow": lax.div(place, wide), "wide": lax.rem(place, wide)}

    barrier = pltpu.get_barrier_semaphore()
    for shift in range(1, count):
        pl.semaphore_signal(
            barrier,
            inc=1,
            device_id=device(lax.rem(me + shift, count)),
            device_id_type=pl.DeviceIdType.MESH,
        )
    pl.semaphore_wait(barrier, count - 1)
    copies = []
    for shift in range(1, count):
        target = lax.rem(me + shift, count)
        copy = pltpu.make_async_remote_copy(
            src_ref=sent.at[target],
            dst_ref=arrived.at[me],
            send_sem=send_sem.at[shift - 1],
            recv_sem=recv_sem.at[shift - 1],
            device_id=device(target),
            device_id_type=pl.DeviceIdType.MESH,
        )
        copy.start()
        copies.append(copy)
    arrived[me] = sent[me]
    for copy in copies:
        copy.wait()


def exchange(blocks, parts, wide, place):
    return pl.pallas_call(
        functools.partial(exchange_kernel, parts, wide),
        out_shape=jax.ShapeDtypeStruct(blocks.shape, BF16),
        in_specs=[pl.BlockSpec(memory_space=pltpu.VMEM)],
        out_specs=pl.BlockSpec(memory_space=pltpu.VMEM),
        scratch_shapes=[
            pltpu.SemaphoreType.DMA((parts * wide - 1,)),
            pltpu.SemaphoreType.DMA((parts * wide - 1,)),
        ],
        compiler_params=pltpu.CompilerParams(collective_id=place, has_side_effects=True),
    )(blocks)


def whole_spec(shape):
    return pl.BlockSpec(shape, lambda *_: (0,) * len(shape))


def body(plume_state, spectral_weight, channel_mixer, channel_bias, upstream_grad):
    row_count, cells_x, cells_y, depth = plume_state.shape
    wide = lax.axis_size("wide")
    parts = lax.axis_size("narrow")
    span_x = cells_x * wide
    span_y = cells_y * parts
    flat = cells_x * cells_y
    lanes = C * cells_x
    targets = parts * wide
    pairs = spectral_weight.shape[1]
    band = 16
    group = max(g for g in range(1, 13) if pairs % g == 0)
    down = 1.0 / math.sqrt(depth)
    z_fwd = z_forward_table(depth, down, down)
    z_fwd_back = z_inverse_table(depth, down, down)
    first, other = 1.0 / math.sqrt(2 * MZ), 2.0 / math.sqrt(2 * MZ)
    z_inv = z_inverse_table(depth, first, other)
    z_inv_back = z_forward_table(depth, first, other)
    y_fwd = y_forward_table(span_y, parts, cells_x, 1.0 / math.sqrt(span_y))
    y_inv = y_inverse_table(span_y, parts, cells_x, 1.0 / math.sqrt(MY))
    y_dual_inv = y_forward_table(span_y, parts, cells_x, 1.0 / math.sqrt(MY))
    y_dual_fwd = y_inverse_table(span_y, parts, cells_x, 1.0 / math.sqrt(span_y))
    x_fwd = const(x_forward_table(span_x, parts, wide, cells_x, 1.0 / math.sqrt(span_x)))
    x_inv = x_inverse_table(span_x, wide, cells_x, 1.0 / math.sqrt(MX))
    scale = 1.0 / math.sqrt(MX)
    x_dual_inv = const(
        np.concatenate(
            [x_forward_table(span_x, parts, wide, cells_x, scale, turn) for turn in (False, True)]
        )
    )
    x_dual_fwd = x_inverse_table(span_x, wide, cells_x, 1.0 / math.sqrt(span_x))
    source_rows = cell_mask(cells_x, 2 * targets)
    mode_rows = cell_mask(cells_x, 2 * MX)
    lane_c = np.arange(lanes) // cells_x
    picks_np = np.arange(C)[:, None] == lane_c[None, :]
    picks = const(picks_np)
    copies_np = np.tile(picks_np.T, (1, OCT))
    copies = const(copies_np)
    shrink = const(copies_np.T)
    octets_np = octet_of_rows()[:, None] == (np.arange(OCT * C) // C)[None, :]
    octets = const(octets_np)
    row_mode = (np.arange(2 * MX) // (2 * OCT)) * OCT + np.arange(2 * MX) % OCT
    octets_t = const((np.arange(MX * C) // C)[:, None] == row_mode[None, :])
    sides_np = np.zeros((2 * lanes, 2 * C))
    sides_np[:lanes, :C] = picks_np.T
    sides_np[lanes:, C:] = picks_np.T
    sides = const(sides_np)
    doubled_np = np.zeros((2 * C, 2 * lanes))
    doubled_np[:C, :lanes] = picks_np
    doubled_np[C:, lanes:] = picks_np
    doubled = const(doubled_np)
    spread = const((np.arange(C * band) // band)[:, None] == np.arange(C)[None, :])
    band_index = np.arange(C * band) % band
    band_mask = const(band_index[:, None] == band_index[None, :])

    params = pltpu.CompilerParams(vmem_limit_bytes=VMEM_LIMIT)
    message = jax.ShapeDtypeStruct((targets, 2, pairs, lanes), BF16)
    held = pltpu.VMEM((lanes * MY, 128), F32)
    turned = pltpu.VMEM((2 * MZ * MY, lanes), F32)
    spectral = pltpu.VMEM((C, flat, depth), F32)
    loose = pltpu.VMEM((targets * 2 * pairs, lanes), F32)
    gathered = pltpu.VMEM((2 * wide * pairs, lanes), F32)
    field = plume_state.reshape(C, flat, depth)
    upstream = upstream_grad.reshape(C, flat, depth)
    weights = spectral_weight.reshape(pairs * MX * C, 2 * C)
    field_shape = jax.ShapeDtypeStruct((C, flat, depth), BF16)
    weight_spec = pl.BlockSpec((group * MX * C, 2 * C), lambda i: (i, 0))
    spectrum_spec = pl.BlockSpec((group, C, 2 * MX), lambda i: (i, 0, 0))

    sent = pl.pallas_call(
        functools.partial(forward_kernel, cells_x),
        out_shape=message,
        scratch_shapes=[held, turned],
        compiler_params=params,
    )(field, y_fwd, z_fwd)
    arrived = exchange(sent, parts, wide, 0)

    operands = (x_fwd, x_inv, source_rows, mode_rows, copies, octets, picks, doubled)
    sent, spectrum_t = pl.pallas_call(
        functools.partial(mix_kernel, cells_x, wide, group),
        grid=(pairs // group,),
        in_specs=[whole_spec(message.shape), weight_spec] + [whole_spec(t.shape) for t in operands],
        out_specs=[whole_spec(message.shape), spectrum_spec],
        out_shape=[message, jax.ShapeDtypeStruct((pairs, C, 2 * MX), BF16)],
        scratch_shapes=[loose, gathered],
        compiler_params=params,
    )(arrived, weights, *operands)
    arrived = exchange(sent, parts, wide, 1)

    layer_out, slope, sent = pl.pallas_call(
        functools.partial(middle_kernel, cells_x, band),
        out_shape=[field_shape, field_shape, message],
        scratch_shapes=[held, turned, spectral],
        compiler_params=params,
    )(
        arrived, field, upstream, spread, channel_mixer.T, band_mask, channel_bias[:, None],
        y_inv, z_inv, y_dual_inv, z_inv_back,
    )
    arrived = exchange(sent, parts, wide, 2)

    operands = (
        x_dual_inv, x_dual_fwd, source_rows, mode_rows, sides, octets, octets_t, shrink,
    )
    sent, weight_grad = pl.pallas_call(
        functools.partial(grad_kernel, cells_x, wide, group),
        grid=(pairs // group,),
        in_specs=[whole_spec(message.shape), weight_spec, spectrum_spec]
        + [whole_spec(t.shape) for t in operands],
        out_specs=[whole_spec(message.shape), weight_spec],
        out_shape=[message, jax.ShapeDtypeStruct(weights.shape, F32)],
        scratch_shapes=[loose, gathered],
        compiler_params=params,
    )(arrived, weights, spectrum_t, *operands)
    arrived = exchange(sent, parts, wide, 3)

    state_grad = pl.pallas_call(
        functools.partial(final_kernel, cells_x, band),
        out_shape=field_shape,
        scratch_shapes=[held, turned, spectral],
        compiler_params=params,
    )(arrived, slope, spread, channel_mixer, band_mask, y_dual_fwd, z_fwd_back)
    return (
        layer_out.reshape(plume_state.shape),
        state_grad.reshape(plume_state.shape),
        weight_grad.reshape(spectral_weight.shape),
    )


def solution(mesh):
    in_specs = (
        P("groups", "wide", "narrow", None),
        P("narrow", "wide", None, None, None),
        P(),
        P(),
        P("groups", "wide", "narrow", None),
    )
    out_specs = (
        P("groups", "wide", "narrow", None),
        P("groups", "wide", "narrow", None),
        P("narrow", "wide", "groups", None, None),
    )
    return jax.shard_map(body, mesh=mesh, in_specs=in_specs, out_specs=out_specs, check_vma=False)
```

```python
import functools
import math

import jax
import jax.numpy as jnp
import numpy as np
from jax import lax
from jax.experimental import pallas as pl
from jax.experimental.pallas import tpu as pltpu
from jax.sharding import PartitionSpec as P

C = 32
MX = 24
MY = 24
MZ = 24
OCT = 8
F32 = jnp.float32
BF16 = jnp.bfloat16
VMEM_LIMIT = 50 * 1024 * 1024


def mm(left, right):
    return jnp.dot(left, right, preferred_element_type=F32)


def mm_nt(left, right):
    return lax.dot_general(left, right, (((1,), (1,)), ((), ())), preferred_element_type=F32)


def const(array):
    return np.asarray(array, np.float32)


class Pack:
    def __init__(self):
        self.rows, self.places = 0, {}
        self.pieces = []

    def add(self, name, table):
        table = table.reshape((-1,) + table.shape[-2:])
        count, rows, columns = table.shape
        held = -(-rows // 16) * 16
        padded = np.zeros((count, held, 256), np.float32)
        padded[:, :rows, :columns] = table
        self.places[name] = (self.rows, held, rows, columns)
        self.pieces.append(padded.reshape(-1, 256))
        self.rows += count * held

    def array(self):
        return jnp.asarray(np.concatenate(self.pieces)).astype(BF16)

    def get(self, ref, name, part=None):
        begin, held, rows, columns = self.places[name]
        if part is None:
            return ref[begin : begin + rows, :columns]
        return ref[pl.ds(pl.multiple_of(begin + part * held, 16), rows), :columns]


def phases(points, frequency):
    turns = np.mod(frequency[:, None] * np.arange(points)[None, :], points)
    return turns.astype(np.float64) * (2.0 * math.pi / points)


def wave(points, modes, sign, scale):
    index = np.arange(modes)
    angles = phases(points, np.where(index < modes // 2, index, index - modes))
    return np.cos(angles) * scale, sign * np.sin(angles) * scale


def y_forward_table(points, parts, cells_x, scale):
    real, imag = wave(points, MY, -1.0, scale)
    local = np.stack([real, imag]).reshape(2, MY, parts, points // parts)
    table = np.einsum("sqnb,ac->nsaqcb", local, np.eye(cells_x))
    return const(table.reshape(parts, 2 * cells_x * MY, -1))


def y_inverse_table(points, parts, cells_x, scale):
    real, imag = wave(points, MY, 1.0, scale)
    local = np.stack([real, -imag]).reshape(2, MY, parts, points // parts)
    table = np.einsum("sqnb,ac->ncbsaq", local, np.eye(cells_x))
    return const(table.reshape(parts, -1, 2 * cells_x * MY))


def half_orders():
    half = np.arange(MZ // 2)
    orders = []
    for first in (0, 1):
        own = np.concatenate([half + first * MZ // 2, half + (1 - first) * MZ // 2])
        orders.append(np.concatenate([own, own + MZ, np.arange(2 * MZ, 128)]))
    return orders


def z_parts(points, first, other):
    angles = phases(points, np.arange(MZ))
    weight = np.where(np.arange(MZ) == 0, first, other)[:, None]
    return np.cos(angles) * weight, np.sin(angles) * weight


def z_forward_table(points, first, other):
    cos, sin = z_parts(points, first, other)
    table = np.zeros((2 * points, 128))
    table[:points, :MZ] = cos.T
    table[points:, :MZ] = sin.T
    table[:points, MZ : 2 * MZ] = -sin.T
    table[points:, MZ : 2 * MZ] = cos.T
    return const(np.stack([table[:, order] for order in half_orders()]))


def z_inverse_table(points, first, other):
    cos, sin = z_parts(points, first, other)
    table = np.zeros((128, 2 * points))
    table[:MZ, :points] = cos
    table[MZ : 2 * MZ, :points] = -sin
    table[:MZ, points:] = sin
    table[MZ : 2 * MZ, points:] = cos
    return const(np.stack([table[order] for order in half_orders()]))


def x_blocks(points, sign, scale):
    real, imag = wave(points, MX, sign, scale)
    table = np.stack([np.stack([real, -imag]), np.stack([imag, real])])
    return table.reshape(2, 2, MX // OCT, OCT, points)


def x_forward_table(points, wide, cells_x, scale, turned=False):
    table = x_blocks(points, -1.0, scale)
    if turned:
        table = np.stack([table[1], -table[0]])
    table = table.reshape(2, 2, MX // OCT, OCT, wide, cells_x)
    return np.einsum("rsjmwa->jrmaws", table).reshape(2 * MX, cells_x * wide * 2)


def x_inverse_table(points, wide, cells_x, scale):
    table = x_blocks(points, 1.0, scale).reshape(2, 2, MX // OCT, OCT, wide, cells_x)
    return const(np.einsum("rsjmwa->wrajsm", table).reshape(wide * 2, cells_x * 2 * MX))


def cell_mask(cells_x, rows):
    owner = np.arange(cells_x * rows) // rows
    return const(owner[:, None] == (np.arange(C * cells_x) % cells_x)[None, :])


def octet_of_rows():
    return np.arange(2 * MX) % OCT


def forward_transform(get_rows, y_table, z_table, held, turned, cells_x):
    rows = cells_x * MY
    together = 4

    def channels(step, carry):
        for offset in range(together):
            c = step * together + offset
            part = mm(y_table, get_rows(c)).astype(BF16)
            both = jnp.concatenate([part[:rows], part[rows:]], axis=1)
            held[pl.ds(pl.multiple_of(c * rows, 8), rows), :] = mm(both, z_table)
        return carry

    lax.fori_loop(0, C // together, channels, 0)
    for q in range(MY):
        block = held[pl.ds(q, C * cells_x, stride=MY), :]
        turned[pl.ds(q, 2 * MZ, stride=MY), :] = block.T[: 2 * MZ]


def inverse_transform(halves, y_table, z_table, put_rows, held, turned, cells_x):
    rows = cells_x * MY
    together = 4
    pairs = halves[0].shape[2]
    points = z_table.shape[1] // 2
    lanes = held.shape[1]
    for half, ref in enumerate(halves):
        for source in range(ref.shape[0]):
            for part in range(2):
                begin = (2 * part + half) * MZ // 2 * MY + source * pairs
                turned[begin : begin + pairs, :] = ref[source, part].astype(F32)
    for q in range(MY):
        block = turned[pl.ds(q, 2 * MZ, stride=MY), :]
        padded = jnp.concatenate([block, jnp.zeros((lanes - 2 * MZ, block.shape[1]), F32)], axis=0)
        held[pl.ds(q, C * cells_x, stride=MY), :] = padded.T

    def channels(step, carry):
        for offset in range(together):
            c = step * together + offset
            block = held[pl.ds(pl.multiple_of(c * rows, 8), rows), :].astype(BF16)
            both = mm(block, z_table).astype(BF16)
            stacked = jnp.concatenate([both[:, :points], both[:, points:]], axis=0)
            put_rows(c, mm(y_table, stacked))
        return carry

    lax.fori_loop(0, C // together, channels, 0)


def tall_mixer(spread, mixer, band, flipped):
    wide = (mm_nt if flipped else mm)(spread, mixer).astype(BF16)
    tall = mm_nt(wide, spread)
    place = lax.broadcasted_iota(jnp.int32, tall.shape, 0) % band
    same = place == lax.broadcasted_iota(jnp.int32, tall.shape, 1) % band
    return jnp.where(same, tall, 0.0).astype(BF16)


def mixed_field(table, field, begin, band):
    depth = field.shape[2]
    blocks = [field[:, pl.ds(begin + half * band, band), :] for half in range(2)]
    flat = [block.reshape(C * band, depth) for block in blocks]
    product = mm(table, jnp.concatenate(flat, axis=1))
    return [product[:, half * depth : (half + 1) * depth].reshape(C, band, depth) for half in range(2)]


def activate(band, field, upstream, table, offset, spectral, layer_out, slope):
    alpha = math.sqrt(2.0 / math.pi)
    cubic = alpha * 0.044715

    def bands(step, carry):
        begin = pl.multiple_of(step * 2 * band, 2 * band)
        linear = mixed_field(table, field, begin, band)
        for half in range(2):
            where = pl.ds(begin + half * band, band)
            v = spectral[:, where, :] + (linear[half] + offset)
            square = v * v
            t = jnp.tanh(v * (alpha + cubic * square))
            gate = 0.5 + 0.5 * t
            layer_out[:, where, :] = (v * gate).astype(BF16)
            rise = (0.5 * v) * (1.0 - t * t) * (alpha + (3.0 * cubic) * square)
            grad = upstream[:, where, :].astype(F32) * (gate + rise)
            slope[:, where, :] = grad.astype(BF16)
        return carry

    lax.fori_loop(0, field.shape[1] // (2 * band), bands, 0)


def final_kernel(pack, cells_x, band, own, other, slope, mixer, tables, out_ref, held, turned, spectral):
    me = lax.axis_index("narrow")

    def put(c, rows):
        spectral[c] = rows

    y_table, z_table = pack.get(tables, "y_back", me), pack.get(tables, "z_back", me)
    inverse_transform((own, other), y_table, z_table, put, held, turned, cells_x)
    table = tall_mixer(pack.get(tables, "spread"), mixer[...], band, False)

    def bands(step, carry):
        begin = pl.multiple_of(step * 2 * band, 2 * band)
        linear = mixed_field(table, slope, begin, band)
        for half in range(2):
            where = pl.ds(begin + half * band, band)
            out_ref[:, where, :] = (spectral[:, where, :] + linear[half]).astype(BF16)
        return carry

    lax.fori_loop(0, slope.shape[1] // (2 * band), bands, 0)


def unpack_pairs(arrived, loose):
    pairs = arrived.shape[2]
    for source in range(arrived.shape[0]):
        for part in range(2):
            begin = (source * 2 + part) * pairs
            loose[begin : begin + pairs, :] = arrived[source, part].astype(F32)


def to_modes(loose, x_table, cell_rows, first, group, pairs, cells_x):
    count = loose.shape[0] // pairs
    blocks = []
    for offset in range(group):
        data = loose[pl.ds(first + offset, count, stride=pairs), :].astype(BF16)
        blocks.append(jnp.concatenate([data] * cells_x, axis=0) * cell_rows)
    return mm(x_table, jnp.concatenate(blocks, axis=1)).astype(BF16)


def from_modes(modes, x_back, cell_rows, gathered, first, group, pairs, cells_x):
    rows = 2 * MX
    lanes = modes.shape[1]
    blocks = []
    for offset in range(group):
        data = modes[offset * rows : (offset + 1) * rows]
        blocks.append(jnp.concatenate([data] * cells_x, axis=0) * cell_rows)
    back = mm(x_back, jnp.concatenate(blocks, axis=1))
    for offset in range(group):
        where = pl.ds(first + offset, x_back.shape[0], stride=pairs)
        gathered[where, :] = back[:, offset * lanes : (offset + 1) * lanes]


def greet(wide):
    barrier = pltpu.get_barrier_semaphore()
    place, core = lax.axis_index("wide"), lax.axis_index("narrow")
    for shift in range(1, wide):
        signal(barrier, {"wide": lax.rem(place + shift, wide)})
    signal(barrier, {"narrow": 1 - core})


def signal(barrier, device):
    pl.semaphore_signal(barrier, inc=1, device_id=device, device_id_type=pl.DeviceIdType.MESH)


def met(wide):
    pl.semaphore_wait(pltpu.get_barrier_semaphore(), wide)


def remote(source, target, sems, index, device):
    return pltpu.make_async_remote_copy(
        src_ref=source,
        dst_ref=target,
        send_sem=sems[0].at[index],
        recv_sem=sems[1].at[index],
        device_id=device,
        device_id_type=pl.DeviceIdType.MESH,
    )


def start_wide(message, arrived, sems, wide):
    place = lax.axis_index("wide")
    copies = []
    for shift in range(1, wide):
        target = lax.rem(place + shift, wide)
        copy = remote(message.at[target], arrived.at[place], sems, shift, {"wide": target})
        copy.start()
        copies.append(copy)
    arrived[place] = message[place]
    return copies


def gather_modes(turned, message, arrived, mate_out, mate_in, sems, mate_sems, wide):
    half = MZ // 2 * MY
    pairs = message.shape[2]
    for part in range(2):
        begin = (2 * part + 1) * half
        mate_out[part] = turned[begin : begin + half, :].astype(BF16)
    swap = remote(mate_out, mate_in, mate_sems, 0, {"narrow": 1 - lax.axis_index("narrow")})
    swap.start()
    swap.wait()
    for part in range(2):
        total = turned[2 * part * half : (2 * part + 1) * half, :] + mate_in[part].astype(F32)
        for target in range(wide):
            begin = target * pairs
            message[target, part] = total[begin : begin + pairs].astype(BF16)
    for copy in start_wide(message, arrived, sems, wide):
        copy.wait()


def scatter_cells(gathered, message, own, other, sems, mate_sems, wide):
    pairs = message.shape[2]
    place, mate = lax.axis_index("wide"), 1 - lax.axis_index("narrow")
    for target in range(wide):
        for part in range(2):
            begin = (target * 2 + part) * pairs
            message[target, part] = gathered[begin : begin + pairs, :].astype(BF16)
    copies = start_wide(message, own, sems, wide)
    passed = [remote(own.at[place], other.at[place], mate_sems, 0, {"narrow": mate})]
    passed[0].start()
    for shift, copy in enumerate(copies, 1):
        copy.wait_recv()
        source = lax.rem(place + wide - shift, wide)
        onward = remote(own.at[source], other.at[source], mate_sems, shift, {"narrow": mate})
        onward.start()
        passed.append(onward)
    for copy in copies:
        copy.wait_send()
    for onward in passed:
        onward.wait()


def per_pair(array, group, low, high):
    lanes = array.shape[1] // group
    parts = [array[low:high, n * lanes : (n + 1) * lanes] for n in range(group)]
    return jnp.concatenate(parts, axis=0)


def weight_rows(weights, pair, j):
    begin = pl.multiple_of(pair * MX * C + j * OCT * C, OCT * C)
    return weights[pl.ds(begin, OCT * C), :]


def mix_pairs(pack, tables, cells_x, group, pairs, first, weights, loose, gathered, spectrum_t):
    rows = 2 * MX
    octets = pack.get(tables, "octets")
    picks = pack.get(tables, "picks")
    modes = to_modes(
        loose, pack.get(tables, "x"), pack.get(tables, "sources"), first, group, pairs, cells_x
    )
    chosen = per_pair(modes, group, 0, rows)
    mask = jnp.concatenate([octets] * group, axis=0)
    diagonal = mm(chosen, pack.get(tables, "copies")).astype(BF16) * mask
    products = []
    for n in range(group * (MX // OCT)):
        block = weight_rows(weights, first + n // (MX // OCT), n % (MX // OCT))
        products.append(mm(diagonal[2 * OCT * n : 2 * OCT * (n + 1)], block))
    product = jnp.concatenate(products, axis=0).astype(BF16)
    both = mm(product, pack.get(tables, "doubled"))
    lanes = both.shape[1] // 2
    mixed = []
    for n in range(group * (MX // OCT)):
        top = both[2 * OCT * n : 2 * OCT * n + OCT]
        bottom = both[2 * OCT * n + OCT : 2 * OCT * (n + 1)]
        mixed.append(top[:, :lanes] - bottom[:, lanes:])
        mixed.append(top[:, lanes:] + bottom[:, :lanes])
    mixed = jnp.concatenate(mixed, axis=0).astype(BF16)
    from_modes(
        mixed, pack.get(tables, "x_back"), pack.get(tables, "modes"), gathered, first, group,
        pairs, cells_x,
    )
    for n in range(group):
        turned = mm_nt(picks, chosen[n * rows : (n + 1) * rows])
        spectrum_t[first + n] = turned.astype(BF16)


def grad_pairs(pack, tables, cells_x, group, pairs, first, weights, loose, gathered, factors):
    rows = 2 * MX
    modes = to_modes(
        loose, pack.get(tables, "x"), pack.get(tables, "sources"), first, group, pairs, cells_x
    )
    straight = per_pair(modes, group, 0, rows)
    turned = per_pair(modes, group, rows, 2 * rows)
    both = jnp.concatenate([straight, turned], axis=1)
    stacked = mm(both, pack.get(tables, "sides")).astype(BF16)
    coeffs = []
    for n in range(group * (MX // OCT)):
        block = weight_rows(weights, first + n // (MX // OCT), n % (MX // OCT))
        coeffs.append(mm_nt(stacked[2 * OCT * n : 2 * OCT * (n + 1)], block))
    mask = jnp.concatenate([pack.get(tables, "octets")] * group, axis=0)
    coeff = jnp.concatenate(coeffs, axis=0).astype(BF16) * mask
    spread = mm(coeff, pack.get(tables, "shrink")).astype(BF16)
    from_modes(
        spread, pack.get(tables, "x_back"), pack.get(tables, "modes"), gathered, first, group,
        pairs, cells_x,
    )
    for n in range(group):
        factors[first + n] = stacked[n * rows : (n + 1) * rows]


def first_kernel(
    pack, cells_x, wide, group, field, weights_hbm, tables, own, other, spectrum_t, held, turned,
    loose, gathered, weights, message, arrived, message_back, mate_out, mate_in, load_sem, *sems,
):
    me = lax.axis_index("narrow")
    pairs = message.shape[2]
    greet(wide)
    load = pltpu.make_async_copy(weights_hbm, weights, load_sem)
    load.start()
    y_table, z_table = pack.get(tables, "y", me), pack.get(tables, "z", me)
    forward_transform(lambda c: field[c], y_table, z_table, held, turned, cells_x)
    met(wide)
    gather_modes(turned, message, arrived, mate_out, mate_in, sems[0:2], sems[2:4], wide)
    unpack_pairs(arrived, loose)
    load.wait()

    def groups(step, carry):
        mix_pairs(
            pack, tables, cells_x, group, pairs, step * group, weights, loose, gathered, spectrum_t
        )
        return carry

    lax.fori_loop(0, pairs // group, groups, 0)
    scatter_cells(gathered, message_back, own, other, sems[4:6], sems[6:8], wide)


def second_kernel(
    pack, cells_x, wide, group, band, own_in, other_in, field, upstream, weights_hbm, mixer, bias,
    tables, layer_out, slope, own, other, factors, held, turned, loose, gathered, weights, message,
    arrived, message_back, mate_out, mate_in, load_sem, spectral, *sems,
):
    me = lax.axis_index("narrow")
    pairs = message.shape[2]
    greet(wide)
    load = pltpu.make_async_copy(weights_hbm, weights, load_sem)
    load.start()

    def put(c, rows):
        spectral[c] = rows

    y_table, z_table = pack.get(tables, "y_back", me), pack.get(tables, "z_back", me)
    inverse_transform((own_in, other_in), y_table, z_table, put, held, turned, cells_x)
    table = tall_mixer(pack.get(tables, "spread"), mixer[...], band, True)
    unit = lax.broadcasted_iota(jnp.int32, (C, C), 0) == lax.broadcasted_iota(jnp.int32, (C, C), 1)
    offset = jnp.sum(jnp.where(unit, bias[...], 0.0), axis=1, keepdims=True)[:, :, None]
    activate(band, field, upstream, table, offset, spectral, layer_out, slope)
    y_table, z_table = pack.get(tables, "y", me), pack.get(tables, "z", me)
    forward_transform(lambda c: slope[c], y_table, z_table, held, turned, cells_x)
    met(wide)
    gather_modes(turned, message, arrived, mate_out, mate_in, sems[0:2], sems[2:4], wide)
    unpack_pairs(arrived, loose)
    load.wait()

    def groups(step, carry):
        grad_pairs(
            pack, tables, cells_x, group, pairs, step * group, weights, loose, gathered, factors
        )
        return carry

    lax.fori_loop(0, pairs // group, groups, 0)
    scatter_cells(gathered, message_back, own, other, sems[4:6], sems[6:8], wide)


def weight_kernel(pack, group, spectrum_t, factors, tables, weight_grad):
    for n in range(group):
        tall = jnp.concatenate([spectrum_t[n]] * MX, axis=0) * pack.get(tables, "octets_t")
        weight_grad[n * MX * C : (n + 1) * MX * C, :] = mm(tall, factors[n])


def whole_spec(shape):
    return pl.BlockSpec(shape, lambda *_: (0,) * len(shape))


def body(plume_state, spectral_weight, channel_mixer, channel_bias, upstream_grad):
    row_count, cells_x, cells_y, depth = plume_state.shape
    wide = lax.axis_size("wide")
    parts = lax.axis_size("narrow")
    span_x = cells_x * wide
    span_y = cells_y * parts
    flat = cells_x * cells_y
    lanes = C * cells_x
    pairs = spectral_weight.shape[1]
    band = 16
    group = max(g for g in range(1, 13) if pairs % g == 0)
    strip = max(g for g in range(1, 7) if pairs % g == 0)
    down = 1.0 / math.sqrt(depth)
    z_fwd = z_forward_table(depth, down, down)
    z_fwd_back = z_inverse_table(depth, down, down)
    first, other = 1.0 / math.sqrt(2 * MZ), 2.0 / math.sqrt(2 * MZ)
    z_inv = z_inverse_table(depth, first, other)
    z_inv_back = z_forward_table(depth, first, other)
    y_fwd = y_forward_table(span_y, parts, cells_x, 1.0 / math.sqrt(span_y))
    y_inv = y_inverse_table(span_y, parts, cells_x, 1.0 / math.sqrt(MY))
    y_dual_inv = y_forward_table(span_y, parts, cells_x, 1.0 / math.sqrt(MY))
    y_dual_fwd = y_inverse_table(span_y, parts, cells_x, 1.0 / math.sqrt(span_y))
    x_fwd = const(x_forward_table(span_x, wide, cells_x, 1.0 / math.sqrt(span_x)))
    x_inv = x_inverse_table(span_x, wide, cells_x, 1.0 / math.sqrt(MX))
    scale = 1.0 / math.sqrt(MX)
    x_dual_inv = const(
        np.concatenate(
            [x_forward_table(span_x, wide, cells_x, scale, turn) for turn in (False, True)]
        )
    )
    x_dual_fwd = x_inverse_table(span_x, wide, cells_x, 1.0 / math.sqrt(span_x))
    source_rows = cell_mask(cells_x, 2 * wide)
    mode_rows = cell_mask(cells_x, 2 * MX)
    lane_c = np.arange(lanes) // cells_x
    picks_np = np.arange(C)[:, None] == lane_c[None, :]
    picks = const(picks_np)
    copies_np = np.tile(picks_np.T, (1, OCT))
    copies = const(copies_np)
    shrink = const(copies_np.T)
    octets_np = octet_of_rows()[:, None] == (np.arange(OCT * C) // C)[None, :]
    octets = const(octets_np)
    row_mode = (np.arange(2 * MX) // (2 * OCT)) * OCT + np.arange(2 * MX) % OCT
    octets_t = const((np.arange(MX * C) // C)[:, None] == row_mode[None, :])
    sides_np = np.zeros((2 * lanes, 2 * C))
    sides_np[:lanes, :C] = picks_np.T
    sides_np[lanes:, C:] = picks_np.T
    sides = const(sides_np)
    doubled_np = np.zeros((2 * C, 2 * lanes))
    doubled_np[:C, :lanes] = picks_np
    doubled_np[C:, lanes:] = picks_np
    doubled = const(doubled_np)
    spread = const((np.arange(C * band) // band)[:, None] == np.arange(C)[None, :])

    params = pltpu.CompilerParams(vmem_limit_bytes=VMEM_LIMIT)
    shape = (wide, 2, pairs, lanes)
    message = jax.ShapeDtypeStruct(shape, BF16)
    held = pltpu.VMEM((lanes * MY, 128), F32)
    turned = pltpu.VMEM((2 * MZ * MY, lanes), F32)
    spectral = pltpu.VMEM((C, flat, depth), F32)
    field = plume_state.reshape(C, flat, depth)
    upstream = upstream_grad.reshape(C, flat, depth)
    weights = spectral_weight.reshape(pairs * MX * C, 2 * C)
    field_shape = jax.ShapeDtypeStruct((C, flat, depth), BF16)
    local = pl.BlockSpec(memory_space=pltpu.VMEM)
    far = pl.BlockSpec(memory_space=pl.ANY)
    mate = pltpu.VMEM((2, MZ // 2 * MY, lanes), BF16)
    work = [
        held,
        turned,
        pltpu.VMEM((wide * 2 * pairs, lanes), F32),
        pltpu.VMEM((2 * wide * pairs, lanes), F32),
        pltpu.VMEM(weights.shape, BF16),
        pltpu.VMEM(shape, BF16),
        pltpu.VMEM(shape, BF16),
        pltpu.VMEM(shape, BF16),
        mate,
        mate,
        pltpu.SemaphoreType.DMA,
    ]
    sems = [pltpu.SemaphoreType.DMA((count,)) for count in (wide, wide, 1, 1) + (wide,) * 4]

    pack = Pack()
    pack.add("y", y_fwd)
    pack.add("z", z_fwd)
    for name, table in (
        ("x", x_fwd), ("x_back", x_inv), ("sources", source_rows), ("modes", mode_rows),
        ("copies", copies), ("octets", octets), ("picks", picks), ("doubled", doubled),
    ):
        pack.add(name, table)
    own, other, spectrum_t = pl.pallas_call(
        functools.partial(first_kernel, pack, cells_x, wide, group),
        in_specs=[local, far, local],
        out_specs=[local] * 3,
        out_shape=[message, message, jax.ShapeDtypeStruct((pairs, C, 2 * MX), BF16)],
        scratch_shapes=work + sems,
        compiler_params=pltpu.CompilerParams(
            vmem_limit_bytes=VMEM_LIMIT, collective_id=0, has_side_effects=True
        ),
    )(field, weights, pack.array())

    pack = Pack()
    pack.add("y", y_dual_inv)
    pack.add("z", z_inv_back)
    pack.add("y_back", y_inv)
    pack.add("z_back", z_inv)
    for name, table in (
        ("x", x_dual_inv), ("x_back", x_dual_fwd), ("sources", source_rows), ("modes", mode_rows),
        ("sides", sides), ("octets", octets), ("shrink", shrink), ("spread", spread),
    ):
        pack.add(name, table)
    layer_out, slope, own, other, factors = pl.pallas_call(
        functools.partial(second_kernel, pack, cells_x, wide, group, band),
        in_specs=[local] * 4 + [far] + [local] * 3,
        out_specs=[local] * 5,
        out_shape=[
            field_shape, field_shape, message, message,
            jax.ShapeDtypeStruct((pairs, 2 * MX, 2 * C), BF16),
        ],
        scratch_shapes=work + [spectral] + sems,
        compiler_params=pltpu.CompilerParams(
            vmem_limit_bytes=VMEM_LIMIT, collective_id=1, has_side_effects=True
        ),
    )(own, other, field, upstream, weights, channel_mixer, channel_bias[None, :], pack.array())

    pack = Pack()
    pack.add("octets_t", octets_t)
    tables = pack.array()
    weight_grad = pl.pallas_call(
        functools.partial(weight_kernel, pack, strip),
        grid=(pairs // (strip),),
        in_specs=[
            pl.BlockSpec((strip, C, 2 * MX), lambda i: (i, 0, 0)),
            pl.BlockSpec((strip, 2 * MX, 2 * C), lambda i: (i, 0, 0)),
            whole_spec(tables.shape),
        ],
        out_specs=pl.BlockSpec(((strip) * MX * C, 2 * C), lambda i: (i, 0)),
        out_shape=jax.ShapeDtypeStruct(weights.shape, F32),
        compiler_params=params,
    )(spectrum_t, factors, tables)

    pack = Pack()
    pack.add("y_back", y_dual_fwd)
    pack.add("z_back", z_fwd_back)
    pack.add("spread", spread)
    state_grad = pl.pallas_call(
        functools.partial(final_kernel, pack, cells_x, band),
        out_shape=field_shape,
        scratch_shapes=[held, turned, spectral],
        compiler_params=params,
    )(own, other, slope, channel_mixer, pack.array())
    return (
        layer_out.reshape(plume_state.shape),
        state_grad.reshape(plume_state.shape),
        weight_grad.reshape(spectral_weight.shape),
    )


def solution(mesh):
    in_specs = (
        P("groups", "wide", "narrow", None),
        P("narrow", "wide", None, None, None),
        P(),
        P(),
        P("groups", "wide", "narrow", None),
    )
    out_specs = (
        P("groups", "wide", "narrow", None),
        P("groups", "wide", "narrow", None),
        P("narrow", "wide", "groups", None, None),
    )
    return jax.shard_map(body, mesh=mesh, in_specs=in_specs, out_specs=out_specs, check_vma=False)
```

```python
import functools
import math

import jax
import jax.numpy as jnp
import numpy as np
from jax import lax
from jax.experimental import pallas as pl
from jax.experimental.pallas import tpu as pltpu
from jax.sharding import PartitionSpec as P

C = 32
MX = 24
MY = 24
MZ = 24
OCT = 8
F32 = jnp.float32
BF16 = jnp.bfloat16
VMEM_LIMIT = 50 * 1024 * 1024


def mm(left, right):
    return jnp.dot(left, right, preferred_element_type=F32)


def mm_nt(left, right):
    return lax.dot_general(left, right, (((1,), (1,)), ((), ())), preferred_element_type=F32)


def const(array):
    return np.asarray(array, np.float32)


class Pack:
    def __init__(self):
        self.rows, self.places = 0, {}
        self.pieces = []

    def add(self, name, table):
        table = table.reshape((-1,) + table.shape[-2:])
        count, rows, columns = table.shape
        held = -(-rows // 16) * 16
        padded = np.zeros((count, held, 256), np.float32)
        padded[:, :rows, :columns] = table
        self.places[name] = (self.rows, held, rows, columns)
        self.pieces.append(padded.reshape(-1, 256))
        self.rows += count * held

    def array(self):
        return jnp.asarray(np.concatenate(self.pieces)).astype(BF16)

    def get(self, ref, name, part=None):
        begin, held, rows, columns = self.places[name]
        if part is None:
            return ref[begin : begin + rows, :columns]
        return ref[pl.ds(pl.multiple_of(begin + part * held, 16), rows), :columns]


def phases(points, frequency):
    turns = np.mod(frequency[:, None] * np.arange(points)[None, :], points)
    return turns.astype(np.float64) * (2.0 * math.pi / points)


def wave(points, modes, sign, scale):
    index = np.arange(modes)
    angles = phases(points, np.where(index < modes // 2, index, index - modes))
    return np.cos(angles) * scale, sign * np.sin(angles) * scale


def y_forward_table(points, parts, cells_x, scale):
    real, imag = wave(points, MY, -1.0, scale)
    local = np.stack([real, imag]).reshape(2, MY, parts, points // parts)
    table = np.einsum("sqnb,ac->nsaqcb", local, np.eye(cells_x))
    return const(table.reshape(parts, 2 * cells_x * MY, -1))


def y_inverse_table(points, parts, cells_x, scale):
    real, imag = wave(points, MY, 1.0, scale)
    local = np.stack([real, -imag]).reshape(2, MY, parts, points // parts)
    table = np.einsum("sqnb,ac->ncbsaq", local, np.eye(cells_x))
    return const(table.reshape(parts, -1, 2 * cells_x * MY))


def half_orders():
    half = np.arange(MZ // 2)
    orders = []
    for first in (0, 1):
        own = np.concatenate([half + first * MZ // 2, half + (1 - first) * MZ // 2])
        orders.append(np.concatenate([own, own + MZ, np.arange(2 * MZ, 128)]))
    return orders


def z_parts(points, first, other):
    angles = phases(points, np.arange(MZ))
    weight = np.where(np.arange(MZ) == 0, first, other)[:, None]
    return np.cos(angles) * weight, np.sin(angles) * weight


def z_forward_table(points, first, other):
    cos, sin = z_parts(points, first, other)
    table = np.zeros((2 * points, 128))
    table[:points, :MZ] = cos.T
    table[points:, :MZ] = sin.T
    table[:points, MZ : 2 * MZ] = -sin.T
    table[points:, MZ : 2 * MZ] = cos.T
    return const(np.stack([table[:, order] for order in half_orders()]))


def z_inverse_table(points, first, other):
    cos, sin = z_parts(points, first, other)
    table = np.zeros((128, 2 * points))
    table[:MZ, :points] = cos
    table[MZ : 2 * MZ, :points] = -sin
    table[:MZ, points:] = sin
    table[MZ : 2 * MZ, points:] = cos
    return const(np.stack([table[order] for order in half_orders()]))


def x_blocks(points, sign, scale):
    real, imag = wave(points, MX, sign, scale)
    table = np.stack([np.stack([real, -imag]), np.stack([imag, real])])
    return table.reshape(2, 2, MX // OCT, OCT, points)


def x_forward_table(points, wide, cells_x, scale, turned=False):
    table = x_blocks(points, -1.0, scale)
    if turned:
        table = np.stack([table[1], -table[0]])
    table = table.reshape(2, 2, MX // OCT, OCT, wide, cells_x)
    return np.einsum("rsjmwa->jrmaws", table).reshape(2 * MX, cells_x * wide * 2)


def x_inverse_table(points, wide, cells_x, scale):
    table = x_blocks(points, 1.0, scale).reshape(2, 2, MX // OCT, OCT, wide, cells_x)
    return const(np.einsum("rsjmwa->wrajsm", table).reshape(wide * 2, cells_x * 2 * MX))


def cell_mask(cells_x, rows):
    owner = np.arange(cells_x * rows) // rows
    return const(owner[:, None] == (np.arange(C * cells_x) % cells_x)[None, :])


def octet_of_rows():
    return np.arange(2 * MX) % OCT


def forward_transform(get_rows, y_table, z_table, held, turned, cells_x):
    rows = cells_x * MY
    together = 16

    def channels(step, carry):
        for offset in range(together):
            c = step * together + offset
            part = mm(y_table, get_rows(c)).astype(BF16)
            both = jnp.concatenate([part[:rows], part[rows:]], axis=1)
            held[pl.ds(pl.multiple_of(c * rows, 8), rows), :] = mm(both, z_table)
        return carry

    lax.fori_loop(0, C // together, channels, 0)
    for q in range(MY):
        block = held[pl.ds(q, C * cells_x, stride=MY), :]
        turned[pl.ds(q, 2 * MZ, stride=MY), :] = block.T[: 2 * MZ]


def inverse_transform(halves, y_table, z_table, put_rows, held, turned, cells_x):
    rows = cells_x * MY
    together = 16
    pairs = halves[0].shape[2]
    points = z_table.shape[1] // 2
    lanes = held.shape[1]
    for half, ref in enumerate(halves):
        for source in range(ref.shape[0]):
            for part in range(2):
                begin = (2 * part + half) * MZ // 2 * MY + source * pairs
                turned[begin : begin + pairs, :] = ref[source, part].astype(F32)
    for q in range(MY):
        block = turned[pl.ds(q, 2 * MZ, stride=MY), :]
        padded = jnp.concatenate([block, jnp.zeros((lanes - 2 * MZ, block.shape[1]), F32)], axis=0)
        held[pl.ds(q, C * cells_x, stride=MY), :] = padded.T

    def channels(step, carry):
        for offset in range(together):
            c = step * together + offset
            block = held[pl.ds(pl.multiple_of(c * rows, 8), rows), :].astype(BF16)
            both = mm(block, z_table).astype(BF16)
            stacked = jnp.concatenate([both[:, :points], both[:, points:]], axis=0)
            put_rows(c, mm(y_table, stacked))
        return carry

    lax.fori_loop(0, C // together, channels, 0)


def tall_mixer(spread, mixer, band, flipped):
    wide = (mm_nt if flipped else mm)(spread, mixer).astype(BF16)
    tall = mm_nt(wide, spread)
    place = lax.broadcasted_iota(jnp.int32, tall.shape, 0) % band
    same = place == lax.broadcasted_iota(jnp.int32, tall.shape, 1) % band
    return jnp.where(same, tall, 0.0).astype(BF16)


def mixed_field(table, field, begin, band):
    depth = field.shape[2]
    blocks = [field[:, pl.ds(begin + half * band, band), :] for half in range(2)]
    flat = [block.reshape(C * band, depth) for block in blocks]
    product = mm(table, jnp.concatenate(flat, axis=1))
    return [product[:, half * depth : (half + 1) * depth].reshape(C, band, depth) for half in range(2)]


def activate(band, field, upstream, table, offset, spectral, layer_out, slope):
    alpha = math.sqrt(2.0 / math.pi)
    cubic = alpha * 0.044715

    def bands(step, carry):
        begin = pl.multiple_of(step * 2 * band, 2 * band)
        linear = mixed_field(table, field, begin, band)
        for half in range(2):
            where = pl.ds(begin + half * band, band)
            v = spectral[:, where, :] + (linear[half] + offset)
            square = v * v
            t = jnp.tanh(v * (alpha + cubic * square))
            gate = 0.5 + 0.5 * t
            layer_out[:, where, :] = (v * gate).astype(BF16)
            rise = (0.5 * v) * (1.0 - t * t) * (alpha + (3.0 * cubic) * square)
            grad = upstream[:, where, :].astype(F32) * (gate + rise)
            slope[:, where, :] = grad.astype(BF16)
        return carry

    lax.fori_loop(0, field.shape[1] // (2 * band), bands, 0)


def mix_gradient(band, slope, table, mixed_grad):
    def bands(step, carry):
        begin = pl.multiple_of(step * 2 * band, 2 * band)
        linear = mixed_field(table, slope, begin, band)
        for half in range(2):
            mixed_grad[:, pl.ds(begin + half * band, band), :] = linear[half].astype(BF16)
        return carry

    lax.fori_loop(0, slope.shape[1] // (2 * band), bands, 0)


def final_kernel(pack, cells_x, own, other, mixed_grad, tables, out_ref, held, turned):
    me = lax.axis_index("narrow")

    def put(c, rows):
        out_ref[c] = (rows + mixed_grad[c].astype(F32)).astype(BF16)

    y_table, z_table = pack.get(tables, "y_back", me), pack.get(tables, "z_back", me)
    inverse_transform((own, other), y_table, z_table, put, held, turned, cells_x)


def unpack_pairs(arrived, loose):
    pairs = arrived.shape[2]
    for source in range(arrived.shape[0]):
        for part in range(2):
            begin = (source * 2 + part) * pairs
            loose[begin : begin + pairs, :] = arrived[source, part].astype(F32)


def to_modes(loose, x_table, cell_rows, first, group, pairs, cells_x):
    count = loose.shape[0] // pairs
    blocks = []
    for offset in range(group):
        data = loose[pl.ds(first + offset, count, stride=pairs), :].astype(BF16)
        blocks.append(jnp.concatenate([data] * cells_x, axis=0) * cell_rows)
    return mm(x_table, jnp.concatenate(blocks, axis=1)).astype(BF16)


def from_modes(modes, x_back, cell_rows, gathered, first, group, pairs, cells_x):
    rows = 2 * MX
    lanes = modes.shape[1]
    blocks = []
    for offset in range(group):
        data = modes[offset * rows : (offset + 1) * rows]
        blocks.append(jnp.concatenate([data] * cells_x, axis=0) * cell_rows)
    back = mm(x_back, jnp.concatenate(blocks, axis=1))
    for offset in range(group):
        where = pl.ds(first + offset, x_back.shape[0], stride=pairs)
        gathered[where, :] = back[:, offset * lanes : (offset + 1) * lanes]


def greet(wide):
    barrier = pltpu.get_barrier_semaphore()
    place, core = lax.axis_index("wide"), lax.axis_index("narrow")
    for shift in range(1, wide):
        signal(barrier, {"wide": lax.rem(place + shift, wide)})
    signal(barrier, {"narrow": 1 - core})


def signal(barrier, device):
    pl.semaphore_signal(barrier, inc=1, device_id=device, device_id_type=pl.DeviceIdType.MESH)


def met(wide):
    pl.semaphore_wait(pltpu.get_barrier_semaphore(), wide)


def remote(source, target, sems, index, device):
    return pltpu.make_async_remote_copy(
        src_ref=source,
        dst_ref=target,
        send_sem=sems[0].at[index],
        recv_sem=sems[1].at[index],
        device_id=device,
        device_id_type=pl.DeviceIdType.MESH,
    )


def start_wide(message, arrived, sems, wide):
    place = lax.axis_index("wide")
    copies = []
    for shift in range(1, wide):
        target = lax.rem(place + shift, wide)
        copy = remote(message.at[target], arrived.at[place], sems, shift, {"wide": target})
        copy.start()
        copies.append(copy)
    arrived[place] = message[place]
    return copies


def gather_modes(
    turned, message, arrived, mate_out, mate_in, sems, mate_sems, wide, meanwhile=None
):
    half = MZ // 2 * MY
    pairs = message.shape[2]
    for part in range(2):
        begin = (2 * part + 1) * half
        mate_out[part] = turned[begin : begin + half, :].astype(BF16)
    swap = remote(mate_out, mate_in, mate_sems, 0, {"narrow": 1 - lax.axis_index("narrow")})
    swap.start()
    swap.wait()
    for part in range(2):
        total = turned[2 * part * half : (2 * part + 1) * half, :] + mate_in[part].astype(F32)
        for target in range(wide):
            begin = target * pairs
            message[target, part] = total[begin : begin + pairs].astype(BF16)
    copies = start_wide(message, arrived, sems, wide)
    if meanwhile is not None:
        meanwhile()
    for copy in copies:
        copy.wait()


def scatter_cells(gathered, message, own, other, sems, mate_sems, wide):
    pairs = message.shape[2]
    place, mate = lax.axis_index("wide"), 1 - lax.axis_index("narrow")
    for target in range(wide):
        for part in range(2):
            begin = (target * 2 + part) * pairs
            message[target, part] = gathered[begin : begin + pairs, :].astype(BF16)
    copies = start_wide(message, own, sems, wide)
    passed = [remote(own.at[place], other.at[place], mate_sems, 0, {"narrow": mate})]
    passed[0].start()
    for shift, copy in enumerate(copies, 1):
        copy.wait_recv()
        source = lax.rem(place + wide - shift, wide)
        onward = remote(own.at[source], other.at[source], mate_sems, shift, {"narrow": mate})
        onward.start()
        passed.append(onward)
    for copy in copies:
        copy.wait_send()
    for onward in passed:
        onward.wait()


def per_pair(array, group, low, high):
    lanes = array.shape[1] // group
    parts = [array[low:high, n * lanes : (n + 1) * lanes] for n in range(group)]
    return jnp.concatenate(parts, axis=0)


def weight_rows(weights, pair, j):
    begin = pl.multiple_of(pair * MX * C + j * OCT * C, OCT * C)
    return weights[pl.ds(begin, OCT * C), :]


def mix_pairs(pack, tables, cells_x, group, pairs, first, weights, loose, gathered, spectrum_t):
    rows = 2 * MX
    octets = pack.get(tables, "octets")
    picks = pack.get(tables, "picks")
    modes = to_modes(
        loose, pack.get(tables, "x"), pack.get(tables, "sources"), first, group, pairs, cells_x
    )
    chosen = per_pair(modes, group, 0, rows)
    mask = jnp.concatenate([octets] * group, axis=0)
    diagonal = mm(chosen, pack.get(tables, "copies")).astype(BF16) * mask
    products = []
    for n in range(group * (MX // OCT)):
        block = weight_rows(weights, first + n // (MX // OCT), n % (MX // OCT))
        products.append(mm(diagonal[2 * OCT * n : 2 * OCT * (n + 1)], block))
    product = jnp.concatenate(products, axis=0).astype(BF16)
    both = mm(product, pack.get(tables, "doubled"))
    lanes = both.shape[1] // 2
    mixed = []
    for n in range(group * (MX // OCT)):
        top = both[2 * OCT * n : 2 * OCT * n + OCT]
        bottom = both[2 * OCT * n + OCT : 2 * OCT * (n + 1)]
        mixed.append(top[:, :lanes] - bottom[:, lanes:])
        mixed.append(top[:, lanes:] + bottom[:, :lanes])
    mixed = jnp.concatenate(mixed, axis=0).astype(BF16)
    from_modes(
        mixed, pack.get(tables, "x_back"), pack.get(tables, "modes"), gathered, first, group,
        pairs, cells_x,
    )
    for n in range(group):
        turned = mm_nt(picks, chosen[n * rows : (n + 1) * rows])
        spectrum_t[first + n] = turned.astype(BF16)


def grad_pairs(pack, tables, cells_x, group, pairs, first, weights, loose, gathered, factors):
    rows = 2 * MX
    modes = to_modes(
        loose, pack.get(tables, "x"), pack.get(tables, "sources"), first, group, pairs, cells_x
    )
    straight = per_pair(modes, group, 0, rows)
    turned = per_pair(modes, group, rows, 2 * rows)
    both = jnp.concatenate([straight, turned], axis=1)
    stacked = mm(both, pack.get(tables, "sides")).astype(BF16)
    coeffs = []
    for n in range(group * (MX // OCT)):
        block = weight_rows(weights, first + n // (MX // OCT), n % (MX // OCT))
        coeffs.append(mm_nt(stacked[2 * OCT * n : 2 * OCT * (n + 1)], block))
    mask = jnp.concatenate([pack.get(tables, "octets")] * group, axis=0)
    coeff = jnp.concatenate(coeffs, axis=0).astype(BF16) * mask
    spread = mm(coeff, pack.get(tables, "shrink")).astype(BF16)
    from_modes(
        spread, pack.get(tables, "x_back"), pack.get(tables, "modes"), gathered, first, group,
        pairs, cells_x,
    )
    for n in range(group):
        factors[first + n] = stacked[n * rows : (n + 1) * rows]


def first_kernel(
    pack, cells_x, wide, group, field, weights_hbm, tables, own, other, spectrum_t, held, turned,
    loose, gathered, weights, message, arrived, message_back, mate_out, mate_in, load_sem, *sems,
):
    me = lax.axis_index("narrow")
    pairs = message.shape[2]
    greet(wide)
    load = pltpu.make_async_copy(weights_hbm, weights, load_sem)
    load.start()
    y_table, z_table = pack.get(tables, "y", me), pack.get(tables, "z", me)
    forward_transform(lambda c: field[c], y_table, z_table, held, turned, cells_x)
    met(wide)
    gather_modes(turned, message, arrived, mate_out, mate_in, sems[0:2], sems[2:4], wide)
    unpack_pairs(arrived, loose)
    load.wait()

    def groups(step, carry):
        mix_pairs(
            pack, tables, cells_x, group, pairs, step * group, weights, loose, gathered, spectrum_t
        )
        return carry

    lax.fori_loop(0, pairs // group, groups, 0)
    scatter_cells(gathered, message_back, own, other, sems[4:6], sems[6:8], wide)


def second_kernel(
    pack, cells_x, wide, group, band, own_in, other_in, field, upstream, weights_hbm, mixer, bias,
    tables, layer_out, mixed_grad, own, other, factors, held, turned, loose, gathered, weights, message,
    arrived, message_back, mate_out, mate_in, load_sem, spectral, slope, *sems,
):
    me = lax.axis_index("narrow")
    pairs = message.shape[2]
    greet(wide)
    load = pltpu.make_async_copy(weights_hbm, weights, load_sem)
    load.start()

    def put(c, rows):
        spectral[c] = rows

    y_table, z_table = pack.get(tables, "y_back", me), pack.get(tables, "z_back", me)
    inverse_transform((own_in, other_in), y_table, z_table, put, held, turned, cells_x)
    table = tall_mixer(pack.get(tables, "spread"), mixer[...], band, True)
    unit = lax.broadcasted_iota(jnp.int32, (C, C), 0) == lax.broadcasted_iota(jnp.int32, (C, C), 1)
    offset = jnp.sum(jnp.where(unit, bias[...], 0.0), axis=1, keepdims=True)[:, :, None]
    activate(band, field, upstream, table, offset, spectral, layer_out, slope)
    y_table, z_table = pack.get(tables, "y", me), pack.get(tables, "z", me)
    forward_transform(lambda c: slope[c], y_table, z_table, held, turned, cells_x)
    met(wide)

    def meanwhile():
        back = tall_mixer(pack.get(tables, "spread"), mixer[...], band, False)
        mix_gradient(band, slope, back, mixed_grad)

    gather_modes(
        turned, message, arrived, mate_out, mate_in, sems[0:2], sems[2:4], wide, meanwhile
    )
    unpack_pairs(arrived, loose)
    load.wait()

    def groups(step, carry):
        grad_pairs(
            pack, tables, cells_x, group, pairs, step * group, weights, loose, gathered, factors
        )
        return carry

    lax.fori_loop(0, pairs // group, groups, 0)
    scatter_cells(gathered, message_back, own, other, sems[4:6], sems[6:8], wide)


def weight_kernel(pack, group, spectrum_t, factors, tables, weight_grad):
    for n in range(group):
        tall = jnp.concatenate([spectrum_t[n]] * MX, axis=0) * pack.get(tables, "octets_t")
        weight_grad[n * MX * C : (n + 1) * MX * C, :] = mm(tall, factors[n])


def whole_spec(shape):
    return pl.BlockSpec(shape, lambda *_: (0,) * len(shape))


def body(plume_state, spectral_weight, channel_mixer, channel_bias, upstream_grad):
    row_count, cells_x, cells_y, depth = plume_state.shape
    wide = lax.axis_size("wide")
    parts = lax.axis_size("narrow")
    span_x = cells_x * wide
    span_y = cells_y * parts
    flat = cells_x * cells_y
    lanes = C * cells_x
    pairs = spectral_weight.shape[1]
    band = 16
    group = max(g for g in range(1, 13) if pairs % g == 0)
    strip = max(g for g in range(1, 7) if pairs % g == 0)
    down = 1.0 / math.sqrt(depth)
    z_fwd = z_forward_table(depth, down, down)
    z_fwd_back = z_inverse_table(depth, down, down)
    first, other = 1.0 / math.sqrt(2 * MZ), 2.0 / math.sqrt(2 * MZ)
    z_inv = z_inverse_table(depth, first, other)
    z_inv_back = z_forward_table(depth, first, other)
    y_fwd = y_forward_table(span_y, parts, cells_x, 1.0 / math.sqrt(span_y))
    y_inv = y_inverse_table(span_y, parts, cells_x, 1.0 / math.sqrt(MY))
    y_dual_inv = y_forward_table(span_y, parts, cells_x, 1.0 / math.sqrt(MY))
    y_dual_fwd = y_inverse_table(span_y, parts, cells_x, 1.0 / math.sqrt(span_y))
    x_fwd = const(x_forward_table(span_x, wide, cells_x, 1.0 / math.sqrt(span_x)))
    x_inv = x_inverse_table(span_x, wide, cells_x, 1.0 / math.sqrt(MX))
    scale = 1.0 / math.sqrt(MX)
    x_dual_inv = const(
        np.concatenate(
            [x_forward_table(span_x, wide, cells_x, scale, turn) for turn in (False, True)]
        )
    )
    x_dual_fwd = x_inverse_table(span_x, wide, cells_x, 1.0 / math.sqrt(span_x))
    source_rows = cell_mask(cells_x, 2 * wide)
    mode_rows = cell_mask(cells_x, 2 * MX)
    lane_c = np.arange(lanes) // cells_x
    picks_np = np.arange(C)[:, None] == lane_c[None, :]
    picks = const(picks_np)
    copies_np = np.tile(picks_np.T, (1, OCT))
    copies = const(copies_np)
    shrink = const(copies_np.T)
    octets_np = octet_of_rows()[:, None] == (np.arange(OCT * C) // C)[None, :]
    octets = const(octets_np)
    row_mode = (np.arange(2 * MX) // (2 * OCT)) * OCT + np.arange(2 * MX) % OCT
    octets_t = const((np.arange(MX * C) // C)[:, None] == row_mode[None, :])
    sides_np = np.zeros((2 * lanes, 2 * C))
    sides_np[:lanes, :C] = picks_np.T
    sides_np[lanes:, C:] = picks_np.T
    sides = const(sides_np)
    doubled_np = np.zeros((2 * C, 2 * lanes))
    doubled_np[:C, :lanes] = picks_np
    doubled_np[C:, lanes:] = picks_np
    doubled = const(doubled_np)
    spread = const((np.arange(C * band) // band)[:, None] == np.arange(C)[None, :])

    params = pltpu.CompilerParams(vmem_limit_bytes=VMEM_LIMIT)
    shape = (wide, 2, pairs, lanes)
    message = jax.ShapeDtypeStruct(shape, BF16)
    held = pltpu.VMEM((lanes * MY, 128), F32)
    turned = pltpu.VMEM((2 * MZ * MY, lanes), F32)
    spectral = pltpu.VMEM((C, flat, depth), F32)
    field = plume_state.reshape(C, flat, depth)
    upstream = upstream_grad.reshape(C, flat, depth)
    weights = spectral_weight.reshape(pairs * MX * C, 2 * C)
    field_shape = jax.ShapeDtypeStruct((C, flat, depth), BF16)
    local = pl.BlockSpec(memory_space=pltpu.VMEM)
    far = pl.BlockSpec(memory_space=pl.ANY)
    mate = pltpu.VMEM((2, MZ // 2 * MY, lanes), BF16)
    work = [
        held,
        turned,
        pltpu.VMEM((wide * 2 * pairs, lanes), F32),
        pltpu.VMEM((2 * wide * pairs, lanes), F32),
        pltpu.VMEM(weights.shape, BF16),
        pltpu.VMEM(shape, BF16),
        pltpu.VMEM(shape, BF16),
        pltpu.VMEM(shape, BF16),
        mate,
        mate,
        pltpu.SemaphoreType.DMA,
    ]
    sems = [pltpu.SemaphoreType.DMA((count,)) for count in (wide, wide, 1, 1) + (wide,) * 4]

    pack = Pack()
    pack.add("y", y_fwd)
    pack.add("z", z_fwd)
    for name, table in (
        ("x", x_fwd), ("x_back", x_inv), ("sources", source_rows), ("modes", mode_rows),
        ("copies", copies), ("octets", octets), ("picks", picks), ("doubled", doubled),
    ):
        pack.add(name, table)
    own, other, spectrum_t = pl.pallas_call(
        functools.partial(first_kernel, pack, cells_x, wide, group),
        in_specs=[local, far, local],
        out_specs=[local] * 3,
        out_shape=[message, message, jax.ShapeDtypeStruct((pairs, C, 2 * MX), BF16)],
        scratch_shapes=work + sems,
        compiler_params=pltpu.CompilerParams(
            vmem_limit_bytes=VMEM_LIMIT, collective_id=0, has_side_effects=True
        ),
    )(field, weights, pack.array())

    pack = Pack()
    pack.add("y", y_dual_inv)
    pack.add("z", z_inv_back)
    pack.add("y_back", y_inv)
    pack.add("z_back", z_inv)
    for name, table in (
        ("x", x_dual_inv), ("x_back", x_dual_fwd), ("sources", source_rows), ("modes", mode_rows),
        ("sides", sides), ("octets", octets), ("shrink", shrink), ("spread", spread),
    ):
        pack.add(name, table)
    layer_out, mixed_grad, own, other, factors = pl.pallas_call(
        functools.partial(second_kernel, pack, cells_x, wide, group, band),
        in_specs=[local] * 4 + [far] + [local] * 3,
        out_specs=[local] * 5,
        out_shape=[
            field_shape, field_shape, message, message,
            jax.ShapeDtypeStruct((pairs, 2 * MX, 2 * C), BF16),
        ],
        scratch_shapes=work + [spectral, pltpu.VMEM((C, flat, depth), BF16)] + sems,
        compiler_params=pltpu.CompilerParams(
            vmem_limit_bytes=VMEM_LIMIT, collective_id=1, has_side_effects=True
        ),
    )(own, other, field, upstream, weights, channel_mixer, channel_bias[None, :], pack.array())

    pack = Pack()
    pack.add("octets_t", octets_t)
    tables = pack.array()
    weight_grad = pl.pallas_call(
        functools.partial(weight_kernel, pack, strip),
        grid=(pairs // (strip),),
        in_specs=[
            pl.BlockSpec((strip, C, 2 * MX), lambda i: (i, 0, 0)),
            pl.BlockSpec((strip, 2 * MX, 2 * C), lambda i: (i, 0, 0)),
            whole_spec(tables.shape),
        ],
        out_specs=pl.BlockSpec(((strip) * MX * C, 2 * C), lambda i: (i, 0)),
        out_shape=jax.ShapeDtypeStruct(weights.shape, F32),
        compiler_params=params,
    )(spectrum_t, factors, tables)

    own, weight_grad = lax.optimization_barrier((own, weight_grad))
    pack = Pack()
    pack.add("y_back", y_dual_fwd)
    pack.add("z_back", z_fwd_back)
    state_grad = pl.pallas_call(
        functools.partial(final_kernel, pack, cells_x),
        out_shape=field_shape,
        scratch_shapes=[held, turned],
        compiler_params=params,
    )(own, other, mixed_grad, pack.array())
    return (
        layer_out.reshape(plume_state.shape),
        state_grad.reshape(plume_state.shape),
        weight_grad.reshape(spectral_weight.shape),
    )


def solution(mesh):
    in_specs = (
        P("groups", "wide", "narrow", None),
        P("narrow", "wide", None, None, None),
        P(),
        P(),
        P("groups", "wide", "narrow", None),
    )
    out_specs = (
        P("groups", "wide", "narrow", None),
        P("groups", "wide", "narrow", None),
        P("narrow", "wide", "groups", None, None),
    )
    return jax.shard_map(body, mesh=mesh, in_specs=in_specs, out_specs=out_specs, check_vma=False)
```

```python
import functools
import math

import jax
import jax.numpy as jnp
import numpy as np
from jax import lax
from jax.experimental import pallas as pl
from jax.experimental.pallas import tpu as pltpu
from jax.sharding import PartitionSpec as P

C = 32
MX = 24
MY = 24
MZ = 24
OCT = 8
F32 = jnp.float32
BF16 = jnp.bfloat16
VMEM_LIMIT = 50 * 1024 * 1024


def mm(left, right):
    return jnp.dot(left, right, preferred_element_type=F32)


def mm_nt(left, right):
    return lax.dot_general(left, right, (((1,), (1,)), ((), ())), preferred_element_type=F32)


def const(array):
    return np.asarray(array, np.float32)


class Pack:
    def __init__(self):
        self.rows, self.places = 0, {}
        self.pieces = []

    def add(self, name, table):
        table = table.reshape((-1,) + table.shape[-2:])
        count, rows, columns = table.shape
        held = -(-rows // 16) * 16
        padded = np.zeros((count, held, 256), np.float32)
        padded[:, :rows, :columns] = table
        self.places[name] = (self.rows, held, rows, columns)
        self.pieces.append(padded.reshape(-1, 256))
        self.rows += count * held

    def array(self):
        return jnp.asarray(np.concatenate(self.pieces)).astype(BF16)

    def get(self, ref, name, part=None):
        begin, held, rows, columns = self.places[name]
        if part is None:
            return ref[begin : begin + rows, :columns]
        return ref[pl.ds(pl.multiple_of(begin + part * held, 16), rows), :columns]


def phases(points, frequency):
    turns = np.mod(frequency[:, None] * np.arange(points)[None, :], points)
    return turns.astype(np.float64) * (2.0 * math.pi / points)


def wave(points, modes, sign, scale):
    index = np.arange(modes)
    angles = phases(points, np.where(index < modes // 2, index, index - modes))
    return np.cos(angles) * scale, sign * np.sin(angles) * scale


def y_forward_table(points, parts, cells_x, scale):
    real, imag = wave(points, MY, -1.0, scale)
    local = np.stack([real, imag]).reshape(2, MY, parts, points // parts)
    table = np.einsum("sqnb,ac->nsaqcb", local, np.eye(cells_x))
    return const(table.reshape(parts, 2 * cells_x * MY, -1))


def y_inverse_table(points, parts, cells_x, scale):
    real, imag = wave(points, MY, 1.0, scale)
    local = np.stack([real, -imag]).reshape(2, MY, parts, points // parts)
    table = np.einsum("sqnb,ac->ncbsaq", local, np.eye(cells_x))
    return const(table.reshape(parts, -1, 2 * cells_x * MY))


def half_orders():
    half = np.arange(MZ // 2)
    orders = []
    for first in (0, 1):
        own = np.concatenate([half + first * MZ // 2, half + (1 - first) * MZ // 2])
        orders.append(np.concatenate([own, own + MZ, np.arange(2 * MZ, 128)]))
    return orders


def z_parts(points, first, other):
    angles = phases(points, np.arange(MZ))
    weight = np.where(np.arange(MZ) == 0, first, other)[:, None]
    return np.cos(angles) * weight, np.sin(angles) * weight


def z_forward_table(points, first, other):
    cos, sin = z_parts(points, first, other)
    table = np.zeros((2 * points, 128))
    table[:points, :MZ] = cos.T
    table[points:, :MZ] = sin.T
    table[:points, MZ : 2 * MZ] = -sin.T
    table[points:, MZ : 2 * MZ] = cos.T
    return const(np.stack([table[:, order] for order in half_orders()]))


def z_inverse_table(points, first, other):
    cos, sin = z_parts(points, first, other)
    table = np.zeros((128, 2 * points))
    table[:MZ, :points] = cos
    table[MZ : 2 * MZ, :points] = -sin
    table[:MZ, points:] = sin
    table[MZ : 2 * MZ, points:] = cos
    return const(np.stack([table[order] for order in half_orders()]))


def x_blocks(points, sign, scale):
    real, imag = wave(points, MX, sign, scale)
    table = np.stack([np.stack([real, -imag]), np.stack([imag, real])])
    return table.reshape(2, 2, MX // OCT, OCT, points)


def x_forward_table(points, wide, cells_x, scale, turned=False):
    table = x_blocks(points, -1.0, scale)
    if turned:
        table = np.stack([table[1], -table[0]])
    table = table.reshape(2, 2, MX // OCT, OCT, wide, cells_x)
    return np.einsum("rsjmwa->jrmaws", table).reshape(2 * MX, cells_x * wide * 2)


def x_inverse_table(points, wide, cells_x, scale):
    table = x_blocks(points, 1.0, scale).reshape(2, 2, MX // OCT, OCT, wide, cells_x)
    return const(np.einsum("rsjmwa->wrajsm", table).reshape(wide * 2, cells_x * 2 * MX))


def cell_mask(cells_x, rows):
    owner = np.arange(cells_x * rows) // rows
    return const(owner[:, None] == (np.arange(C * cells_x) % cells_x)[None, :])


def octet_of_rows():
    return np.arange(2 * MX) % OCT


def forward_transform(get_rows, y_table, z_table, held, turned, cells_x):
    rows = cells_x * MY
    together = 16

    def channels(step, carry):
        for offset in range(together):
            c = step * together + offset
            part = mm(y_table, get_rows(c)).astype(BF16)
            both = jnp.concatenate([part[:rows], part[rows:]], axis=1)
            held[pl.ds(pl.multiple_of(c * rows, 8), rows), :] = mm(both, z_table)
        return carry

    lax.fori_loop(0, C // together, channels, 0)
    for q in range(MY):
        block = held[pl.ds(q, C * cells_x, stride=MY), :]
        turned[pl.ds(q, 2 * MZ, stride=MY), :] = block.T[: 2 * MZ]


def inverse_transform(halves, y_table, z_table, put_rows, held, turned, cells_x):
    rows = cells_x * MY
    together = 16
    pairs = halves[0].shape[2]
    points = z_table.shape[1] // 2
    lanes = held.shape[1]
    for half, ref in enumerate(halves):
        for source in range(ref.shape[0]):
            for part in range(2):
                begin = (2 * part + half) * MZ // 2 * MY + source * pairs
                turned[begin : begin + pairs, :] = ref[source, part].astype(F32)
    for q in range(MY):
        block = turned[pl.ds(q, 2 * MZ, stride=MY), :]
        padded = jnp.concatenate([block, jnp.zeros((lanes - 2 * MZ, block.shape[1]), F32)], axis=0)
        held[pl.ds(q, C * cells_x, stride=MY), :] = padded.T

    def channels(step, carry):
        for offset in range(together):
            c = step * together + offset
            block = held[pl.ds(pl.multiple_of(c * rows, 8), rows), :].astype(BF16)
            both = mm(block, z_table).astype(BF16)
            stacked = jnp.concatenate([both[:, :points], both[:, points:]], axis=0)
            put_rows(c, mm(y_table, stacked))
        return carry

    lax.fori_loop(0, C // together, channels, 0)


def tall_mixer(spread, mixer, band, flipped):
    wide = (mm_nt if flipped else mm)(spread, mixer).astype(BF16)
    tall = mm_nt(wide, spread)
    place = lax.broadcasted_iota(jnp.int32, tall.shape, 0) % band
    same = place == lax.broadcasted_iota(jnp.int32, tall.shape, 1) % band
    return jnp.where(same, tall, 0.0).astype(BF16)


def mixed_field(table, field, begin, band):
    depth = field.shape[2]
    blocks = [field[:, pl.ds(begin + half * band, band), :] for half in range(2)]
    flat = [block.reshape(C * band, depth) for block in blocks]
    product = mm(table, jnp.concatenate(flat, axis=1))
    return [product[:, half * depth : (half + 1) * depth].reshape(C, band, depth) for half in range(2)]


def mix_state(band, field, table, offset, spectral):
    def bands(step, carry):
        begin = pl.multiple_of(step * 2 * band, 2 * band)
        linear = mixed_field(table, field, begin, band)
        for half in range(2):
            spectral[:, pl.ds(begin + half * band, band), :] = linear[half] + offset
        return carry

    lax.fori_loop(0, field.shape[1] // (2 * band), bands, 0)


def activate(band, upstream, spectral, layer_out, slope):
    alpha = math.sqrt(2.0 / math.pi)
    cubic = alpha * 0.044715

    def bands(step, carry):
        begin = pl.multiple_of(step * 2 * band, 2 * band)
        for half in range(2):
            where = pl.ds(begin + half * band, band)
            v = spectral[:, where, :]
            square = v * v
            t = jnp.tanh(v * (alpha + cubic * square))
            gate = 0.5 + 0.5 * t
            layer_out[:, where, :] = (v * gate).astype(BF16)
            rise = (0.5 * v) * (1.0 - t * t) * (alpha + (3.0 * cubic) * square)
            grad = upstream[:, where, :].astype(F32) * (gate + rise)
            slope[:, where, :] = grad.astype(BF16)
        return carry

    lax.fori_loop(0, upstream.shape[1] // (2 * band), bands, 0)


def mix_gradient(band, slope, table, mixed_grad):
    def bands(step, carry):
        begin = pl.multiple_of(step * 2 * band, 2 * band)
        linear = mixed_field(table, slope, begin, band)
        for half in range(2):
            mixed_grad[:, pl.ds(begin + half * band, band), :] = linear[half].astype(BF16)
        return carry

    lax.fori_loop(0, slope.shape[1] // (2 * band), bands, 0)


def final_kernel(pack, cells_x, own, other, mixed_grad, tables, out_ref, held, turned):
    me = lax.axis_index("narrow")

    def put(c, rows):
        out_ref[c] = (rows + mixed_grad[c].astype(F32)).astype(BF16)

    y_table, z_table = pack.get(tables, "y_back", me), pack.get(tables, "z_back", me)
    inverse_transform((own, other), y_table, z_table, put, held, turned, cells_x)


def unpack_pairs(arrived, loose):
    pairs = arrived.shape[2]
    for source in range(arrived.shape[0]):
        for part in range(2):
            begin = (source * 2 + part) * pairs
            loose[begin : begin + pairs, :] = arrived[source, part].astype(F32)


def to_modes(loose, x_table, cell_rows, first, group, pairs, cells_x):
    count = loose.shape[0] // pairs
    blocks = []
    for offset in range(group):
        data = loose[pl.ds(first + offset, count, stride=pairs), :].astype(BF16)
        blocks.append(jnp.concatenate([data] * cells_x, axis=0) * cell_rows)
    return mm(x_table, jnp.concatenate(blocks, axis=1)).astype(BF16)


def from_modes(modes, x_back, cell_rows, gathered, first, group, pairs, cells_x):
    rows = 2 * MX
    lanes = modes.shape[1]
    blocks = []
    for offset in range(group):
        data = modes[offset * rows : (offset + 1) * rows]
        blocks.append(jnp.concatenate([data] * cells_x, axis=0) * cell_rows)
    back = mm(x_back, jnp.concatenate(blocks, axis=1))
    for offset in range(group):
        where = pl.ds(first + offset, x_back.shape[0], stride=pairs)
        gathered[where, :] = back[:, offset * lanes : (offset + 1) * lanes]


def greet(wide):
    barrier = pltpu.get_barrier_semaphore()
    place, core = lax.axis_index("wide"), lax.axis_index("narrow")
    for shift in range(1, wide):
        signal(barrier, {"wide": lax.rem(place + shift, wide)})
    signal(barrier, {"narrow": 1 - core})


def signal(barrier, device):
    pl.semaphore_signal(barrier, inc=1, device_id=device, device_id_type=pl.DeviceIdType.MESH)


def met(wide):
    pl.semaphore_wait(pltpu.get_barrier_semaphore(), wide)


def remote(source, target, sems, index, device):
    return pltpu.make_async_remote_copy(
        src_ref=source,
        dst_ref=target,
        send_sem=sems[0].at[index],
        recv_sem=sems[1].at[index],
        device_id=device,
        device_id_type=pl.DeviceIdType.MESH,
    )


def start_wide(message, arrived, sems, wide):
    place = lax.axis_index("wide")
    copies = []
    for shift in range(1, wide):
        target = lax.rem(place + shift, wide)
        copy = remote(message.at[target], arrived.at[place], sems, shift, {"wide": target})
        copy.start()
        copies.append(copy)
    arrived[place] = message[place]
    return copies


def gather_modes(
    turned, message, arrived, mate_out, mate_in, sems, mate_sems, wide, meanwhile=None
):
    half = MZ // 2 * MY
    pairs = message.shape[2]
    for part in range(2):
        begin = (2 * part + 1) * half
        mate_out[part] = turned[begin : begin + half, :].astype(BF16)
    swap = remote(mate_out, mate_in, mate_sems, 0, {"narrow": 1 - lax.axis_index("narrow")})
    swap.start()
    swap.wait()
    for part in range(2):
        total = turned[2 * part * half : (2 * part + 1) * half, :] + mate_in[part].astype(F32)
        for target in range(wide):
            begin = target * pairs
            message[target, part] = total[begin : begin + pairs].astype(BF16)
    copies = start_wide(message, arrived, sems, wide)
    if meanwhile is not None:
        meanwhile()
    for copy in copies:
        copy.wait()


def scatter_cells(gathered, message, own, other, sems, mate_sems, wide):
    pairs = message.shape[2]
    place, mate = lax.axis_index("wide"), 1 - lax.axis_index("narrow")
    for target in range(wide):
        for part in range(2):
            begin = (target * 2 + part) * pairs
            message[target, part] = gathered[begin : begin + pairs, :].astype(BF16)
    copies = start_wide(message, own, sems, wide)
    passed = [remote(own.at[place], other.at[place], mate_sems, 0, {"narrow": mate})]
    passed[0].start()
    for shift, copy in enumerate(copies, 1):
        copy.wait_recv()
        source = lax.rem(place + wide - shift, wide)
        onward = remote(own.at[source], other.at[source], mate_sems, shift, {"narrow": mate})
        onward.start()
        passed.append(onward)
    for copy in copies:
        copy.wait_send()
    for onward in passed:
        onward.wait()


def per_pair(array, group, low, high):
    lanes = array.shape[1] // group
    parts = [array[low:high, n * lanes : (n + 1) * lanes] for n in range(group)]
    return jnp.concatenate(parts, axis=0)


def weight_rows(weights, pair, j):
    begin = pl.multiple_of(pair * MX * C + j * OCT * C, OCT * C)
    return weights[pl.ds(begin, OCT * C), :]


def mix_pairs(pack, tables, cells_x, group, pairs, first, weights, loose, gathered, spectrum_t):
    rows = 2 * MX
    octets = pack.get(tables, "octets")
    picks = pack.get(tables, "picks")
    modes = to_modes(
        loose, pack.get(tables, "x"), pack.get(tables, "sources"), first, group, pairs, cells_x
    )
    chosen = per_pair(modes, group, 0, rows)
    mask = jnp.concatenate([octets] * group, axis=0)
    diagonal = mm(chosen, pack.get(tables, "copies")).astype(BF16) * mask
    products = []
    for n in range(group * (MX // OCT)):
        block = weight_rows(weights, first + n // (MX // OCT), n % (MX // OCT))
        products.append(mm(diagonal[2 * OCT * n : 2 * OCT * (n + 1)], block))
    product = jnp.concatenate(products, axis=0).astype(BF16)
    both = mm(product, pack.get(tables, "doubled"))
    lanes = both.shape[1] // 2
    mixed = []
    for n in range(group * (MX // OCT)):
        top = both[2 * OCT * n : 2 * OCT * n + OCT]
        bottom = both[2 * OCT * n + OCT : 2 * OCT * (n + 1)]
        mixed.append(top[:, :lanes] - bottom[:, lanes:])
        mixed.append(top[:, lanes:] + bottom[:, :lanes])
    mixed = jnp.concatenate(mixed, axis=0).astype(BF16)
    from_modes(
        mixed, pack.get(tables, "x_back"), pack.get(tables, "modes"), gathered, first, group,
        pairs, cells_x,
    )
    for n in range(group):
        turned = mm_nt(picks, chosen[n * rows : (n + 1) * rows])
        spectrum_t[first + n] = turned.astype(BF16)


def grad_pairs(pack, tables, cells_x, group, pairs, first, weights, loose, gathered, factors):
    rows = 2 * MX
    modes = to_modes(
        loose, pack.get(tables, "dual_x"), pack.get(tables, "sources"), first, group, pairs, cells_x
    )
    straight = per_pair(modes, group, 0, rows)
    turned = per_pair(modes, group, rows, 2 * rows)
    both = jnp.concatenate([straight, turned], axis=1)
    stacked = mm(both, pack.get(tables, "sides")).astype(BF16)
    coeffs = []
    for n in range(group * (MX // OCT)):
        block = weight_rows(weights, first + n // (MX // OCT), n % (MX // OCT))
        coeffs.append(mm_nt(stacked[2 * OCT * n : 2 * OCT * (n + 1)], block))
    mask = jnp.concatenate([pack.get(tables, "octets")] * group, axis=0)
    coeff = jnp.concatenate(coeffs, axis=0).astype(BF16) * mask
    spread = mm(coeff, pack.get(tables, "shrink")).astype(BF16)
    from_modes(
        spread, pack.get(tables, "dual_x_back"), pack.get(tables, "modes"), gathered, first, group,
        pairs, cells_x,
    )
    for n in range(group):
        factors[first + n] = stacked[n * rows : (n + 1) * rows]


def layer_kernel(
    pack, cells_x, wide, group, band, field, upstream, weights_hbm, mixer, bias, tables, layer_out,
    mixed_grad, own, other, factors, spectrum_t, held, turned, loose, gathered, weights, load_sem,
    spectral, slope, own_state, other_state, *rest,
):
    me = lax.axis_index("narrow")
    buffers, sems = rest[:10], rest[10:]
    pairs = own.shape[2]
    greet(wide)
    load = pltpu.make_async_copy(weights_hbm, weights, load_sem)
    load.start()
    y_table, z_table = pack.get(tables, "y", me), pack.get(tables, "z", me)
    forward_transform(lambda c: field[c], y_table, z_table, held, turned, cells_x)
    met(wide)

    def mix_ahead():
        table = tall_mixer(pack.get(tables, "spread"), mixer[...], band, True)
        rows = lax.broadcasted_iota(jnp.int32, (C, C), 0)
        unit = rows == lax.broadcasted_iota(jnp.int32, (C, C), 1)
        offset = jnp.sum(jnp.where(unit, bias[...], 0.0), axis=1, keepdims=True)[:, :, None]
        mix_state(band, field, table, offset, spectral)

    message, arrived, back, mate_out, mate_in = buffers[:5]
    gather_modes(
        turned, message, arrived, mate_out, mate_in, sems[0:2], sems[2:4], wide, mix_ahead
    )
    unpack_pairs(arrived, loose)
    load.wait()

    def groups(step, carry):
        mix_pairs(
            pack, tables, cells_x, group, pairs, step * group, weights, loose, gathered, spectrum_t
        )
        return carry

    lax.fori_loop(0, pairs // group, groups, 0)
    scatter_cells(gathered, back, own_state, other_state, sems[4:6], sems[6:8], wide)

    def put(c, rows):
        spectral[c] = spectral[c] + rows

    y_table, z_table = pack.get(tables, "y_back", me), pack.get(tables, "z_back", me)
    inverse_transform((own_state, other_state), y_table, z_table, put, held, turned, cells_x)
    activate(band, upstream, spectral, layer_out, slope)
    y_table, z_table = pack.get(tables, "dual_y", me), pack.get(tables, "dual_z", me)
    forward_transform(lambda c: slope[c], y_table, z_table, held, turned, cells_x)

    def mix_back():
        table = tall_mixer(pack.get(tables, "spread"), mixer[...], band, False)
        mix_gradient(band, slope, table, mixed_grad)

    message, arrived, back, mate_out, mate_in = buffers[5:]
    gather_modes(
        turned, message, arrived, mate_out, mate_in, sems[8:10], sems[10:12], wide, mix_back
    )
    unpack_pairs(arrived, loose)

    def grad_groups(step, carry):
        grad_pairs(
            pack, tables, cells_x, group, pairs, step * group, weights, loose, gathered, factors
        )
        return carry

    lax.fori_loop(0, pairs // group, grad_groups, 0)
    scatter_cells(gathered, back, own, other, sems[12:14], sems[14:16], wide)


def weight_kernel(pack, group, spectrum_t, factors, tables, weight_grad):
    for n in range(group):
        tall = jnp.concatenate([spectrum_t[n]] * MX, axis=0) * pack.get(tables, "octets_t")
        weight_grad[n * MX * C : (n + 1) * MX * C, :] = mm(tall, factors[n])


def whole_spec(shape):
    return pl.BlockSpec(shape, lambda *_: (0,) * len(shape))


def body(plume_state, spectral_weight, channel_mixer, channel_bias, upstream_grad):
    row_count, cells_x, cells_y, depth = plume_state.shape
    wide = lax.axis_size("wide")
    parts = lax.axis_size("narrow")
    span_x = cells_x * wide
    span_y = cells_y * parts
    flat = cells_x * cells_y
    lanes = C * cells_x
    pairs = spectral_weight.shape[1]
    band = 16
    group = max(g for g in range(1, 13) if pairs % g == 0)
    strip = max(g for g in range(1, 7) if pairs % g == 0)
    down = 1.0 / math.sqrt(depth)
    z_fwd = z_forward_table(depth, down, down)
    z_fwd_back = z_inverse_table(depth, down, down)
    first, other = 1.0 / math.sqrt(2 * MZ), 2.0 / math.sqrt(2 * MZ)
    z_inv = z_inverse_table(depth, first, other)
    z_inv_back = z_forward_table(depth, first, other)
    y_fwd = y_forward_table(span_y, parts, cells_x, 1.0 / math.sqrt(span_y))
    y_inv = y_inverse_table(span_y, parts, cells_x, 1.0 / math.sqrt(MY))
    y_dual_inv = y_forward_table(span_y, parts, cells_x, 1.0 / math.sqrt(MY))
    y_dual_fwd = y_inverse_table(span_y, parts, cells_x, 1.0 / math.sqrt(span_y))
    x_fwd = const(x_forward_table(span_x, wide, cells_x, 1.0 / math.sqrt(span_x)))
    x_inv = x_inverse_table(span_x, wide, cells_x, 1.0 / math.sqrt(MX))
    scale = 1.0 / math.sqrt(MX)
    x_dual_inv = const(
        np.concatenate(
            [x_forward_table(span_x, wide, cells_x, scale, turn) for turn in (False, True)]
        )
    )
    x_dual_fwd = x_inverse_table(span_x, wide, cells_x, 1.0 / math.sqrt(span_x))
    source_rows = cell_mask(cells_x, 2 * wide)
    mode_rows = cell_mask(cells_x, 2 * MX)
    lane_c = np.arange(lanes) // cells_x
    picks_np = np.arange(C)[:, None] == lane_c[None, :]
    picks = const(picks_np)
    copies_np = np.tile(picks_np.T, (1, OCT))
    copies = const(copies_np)
    shrink = const(copies_np.T)
    octets_np = octet_of_rows()[:, None] == (np.arange(OCT * C) // C)[None, :]
    octets = const(octets_np)
    row_mode = (np.arange(2 * MX) // (2 * OCT)) * OCT + np.arange(2 * MX) % OCT
    octets_t = const((np.arange(MX * C) // C)[:, None] == row_mode[None, :])
    sides_np = np.zeros((2 * lanes, 2 * C))
    sides_np[:lanes, :C] = picks_np.T
    sides_np[lanes:, C:] = picks_np.T
    sides = const(sides_np)
    doubled_np = np.zeros((2 * C, 2 * lanes))
    doubled_np[:C, :lanes] = picks_np
    doubled_np[C:, lanes:] = picks_np
    doubled = const(doubled_np)
    spread = const((np.arange(C * band) // band)[:, None] == np.arange(C)[None, :])

    params = pltpu.CompilerParams(vmem_limit_bytes=VMEM_LIMIT)
    shape = (wide, 2, pairs, lanes)
    message = jax.ShapeDtypeStruct(shape, BF16)
    held = pltpu.VMEM((lanes * MY, 128), F32)
    turned = pltpu.VMEM((2 * MZ * MY, lanes), F32)
    spectral = pltpu.VMEM((C, flat, depth), F32)
    field = plume_state.reshape(C, flat, depth)
    upstream = upstream_grad.reshape(C, flat, depth)
    weights = spectral_weight.reshape(pairs * MX * C, 2 * C)
    field_shape = jax.ShapeDtypeStruct((C, flat, depth), BF16)
    local = pl.BlockSpec(memory_space=pltpu.VMEM)
    far = pl.BlockSpec(memory_space=pl.ANY)
    mate = pltpu.VMEM((2, MZ // 2 * MY, lanes), BF16)
    block = pltpu.VMEM(shape, BF16)
    buffers = [block, block, block, mate, mate]
    sems = [pltpu.SemaphoreType.DMA((count,)) for count in (wide, wide, 1, 1) + (wide,) * 4]
    work = [
        held,
        turned,
        pltpu.VMEM((wide * 2 * pairs, lanes), F32),
        pltpu.VMEM((2 * wide * pairs, lanes), F32),
        pltpu.VMEM(weights.shape, BF16),
        pltpu.SemaphoreType.DMA,
        spectral,
        pltpu.VMEM((C, flat, depth), BF16),
        block,
        block,
    ]

    pack = Pack()
    for name, table in (
        ("y", y_fwd), ("z", z_fwd), ("y_back", y_inv), ("z_back", z_inv), ("dual_y", y_dual_inv),
        ("dual_z", z_inv_back), ("x", x_fwd), ("x_back", x_inv), ("dual_x", x_dual_inv),
        ("dual_x_back", x_dual_fwd), ("sources", source_rows), ("modes", mode_rows),
        ("copies", copies), ("octets", octets), ("picks", picks), ("doubled", doubled),
        ("sides", sides), ("shrink", shrink), ("spread", spread),
    ):
        pack.add(name, table)
    layer_out, mixed_grad, own, other, factors, spectrum_t = pl.pallas_call(
        functools.partial(layer_kernel, pack, cells_x, wide, group, band),
        in_specs=[local] * 2 + [far] + [local] * 3,
        out_specs=[local] * 6,
        out_shape=[
            field_shape, field_shape, message, message,
            jax.ShapeDtypeStruct((pairs, 2 * MX, 2 * C), BF16),
            jax.ShapeDtypeStruct((pairs, C, 2 * MX), BF16),
        ],
        scratch_shapes=work + buffers * 2 + sems * 2,
        compiler_params=pltpu.CompilerParams(
            vmem_limit_bytes=VMEM_LIMIT, collective_id=0, has_side_effects=True
        ),
    )(field, upstream, weights, channel_mixer, channel_bias[None, :], pack.array())

    pack = Pack()
    pack.add("octets_t", octets_t)
    tables = pack.array()
    weight_grad = pl.pallas_call(
        functools.partial(weight_kernel, pack, strip),
        grid=(pairs // (strip),),
        in_specs=[
            pl.BlockSpec((strip, C, 2 * MX), lambda i: (i, 0, 0)),
            pl.BlockSpec((strip, 2 * MX, 2 * C), lambda i: (i, 0, 0)),
            whole_spec(tables.shape),
        ],
        out_specs=pl.BlockSpec(((strip) * MX * C, 2 * C), lambda i: (i, 0)),
        out_shape=jax.ShapeDtypeStruct(weights.shape, F32),
        compiler_params=params,
    )(spectrum_t, factors, tables)

    own, weight_grad = lax.optimization_barrier((own, weight_grad))
    pack = Pack()
    pack.add("y_back", y_dual_fwd)
    pack.add("z_back", z_fwd_back)
    state_grad = pl.pallas_call(
        functools.partial(final_kernel, pack, cells_x),
        out_shape=field_shape,
        scratch_shapes=[held, turned],
        compiler_params=params,
    )(own, other, mixed_grad, pack.array())
    return (
        layer_out.reshape(plume_state.shape),
        state_grad.reshape(plume_state.shape),
        weight_grad.reshape(spectral_weight.shape),
    )


def solution(mesh):
    in_specs = (
        P("groups", "wide", "narrow", None),
        P("narrow", "wide", None, None, None),
        P(),
        P(),
        P("groups", "wide", "narrow", None),
    )
    out_specs = (
        P("groups", "wide", "narrow", None),
        P("groups", "wide", "narrow", None),
        P("narrow", "wide", "groups", None, None),
    )
    return jax.shard_map(body, mesh=mesh, in_specs=in_specs, out_specs=out_specs, check_vma=False)
```
